512 devices in a mesh: hier: 256 (over x_lo, z, y, core), rep: 2 (over x_hi).
Axes of the slice: x: 4 (x_hi: 2, x_lo: 2; x = x_hi * 2 + x_lo), y: 4, z: 16, core: 2. Of those that a mesh axis runs over, the one named last changes fastest.
Arguments:
- rho_real: float32 [512, 256, 256], P('hier', 'rep'), may hold values from -6 to 6
- rho_imag: float32 [512, 256, 256], P('hier', 'rep'), may hold values from -6 to 6
- ham: bfloat16 [2, 256, 256], replicated, as said below
- couple: bfloat16 [12, 256, 256], replicated, as said below
- rates: float32 [12], replicated, may hold values from 0.1 to 2
- coeff_real: float32 [12], replicated, may hold values from 0.2 to 1.5
- coeff_imag: float32 [12], replicated, may hold values from -1 to 1
- occupation: int32 [512, 12], P('hier'), may hold values from 0 to 2, as said below
- upper: int32 [512, 12], P('hier'), may hold values from -1 to 511, as said below
- lower: int32 [512, 12], P('hier'), may hold values from -1 to 511, as said below
Outputs:
- new_real: float32 [512, 256, 256], P('hier', 'rep')
- new_imag: float32 [512, 256, 256], P('hier', 'rep')
The draws below stay inside these ranges and needn't reach their ends.
Inputs may be any that keep to these rules, and one draw needn't show every extreme that they name: `occupation`: each row is the multi-index of one matrix. The window holds all tuples base + b, where b is 0 or 1 in each of 9 modes and 0 elsewhere, and base is 1 in one of those modes and 0 elsewhere; bit j of a matrix's index is b in the j-th of those modes, the same assignment for all rows. upper[a, k] is the matrix whose tuple is occupation[a] plus one in mode k, or -1 where that tuple lies outside the window; such a matrix's index differs from a in exactly one bit, and for each bit every matrix finds the matrix across that bit in exactly one of upper or lower. lower[a, k] is the matrix whose tuple is occupation[a] minus one in mode k, or -1 where that tuple lies outside the window; such a matrix's index differs from a in exactly one bit. ham[0] is symmetric and ham[1] antisymmetric. Each couple[k] is symmetric.
All inputs are finite; a program needn't handle non-finite values.
Results may differ from the reference program's by a relative error of at most 0.0055.
Values may be sent and summed in bfloat16 or wider, within the bound.
No kernel may reach another device: no remote copies, remote signals or barrier semaphores. Data moves between devices by JAX's collectives and lax.ppermute only.
A program may use at most 64 MiB of HBM per device.

```python
import math
import jax
import jax.numpy as jnp
from jax import lax

LEVELS = 256
MODES = 12
WIN_BITS = 9
AUX = 512


def hierarchy_tables(key):
    perm_key = jax.random.fold_in(key, 11)
    lift_key = jax.random.fold_in(key, 12)
    ordering = jax.random.permutation(perm_key, MODES).astype(jnp.int32)
    bit_mode = ordering[:WIN_BITS]
    lifted = bit_mode[jax.random.randint(lift_key, (), 0, WIN_BITS)]
    positions = jnp.arange(AUX, dtype=jnp.int32)
    bit_shifts = jnp.arange(WIN_BITS, dtype=jnp.int32)
    digits = jnp.bitwise_and(jnp.right_shift(positions[:, None], bit_shifts[None, :]), 1)
    mode_range = jnp.arange(MODES, dtype=jnp.int32)
    mode_onehot = (bit_mode[:, None] == mode_range[None, :]).astype(jnp.int32)
    base_lift = (mode_range == lifted).astype(jnp.int32)
    occupation = jnp.dot(digits, mode_onehot) + base_lift[None, :]
    partners = jnp.bitwise_xor(positions[:, None], jnp.left_shift(jnp.int32(1), bit_shifts)[None, :])
    up_plus = jnp.where(digits == 0, partners + 1, 0)
    down_plus = jnp.where(digits == 1, partners + 1, 0)
    return (occupation, jnp.dot(up_plus, mode_onehot) - 1, jnp.dot(down_plus, mode_onehot) - 1)


def draw_occupation(key, part):
    tables = hierarchy_tables(key)
    return tables[0]


def draw_upper(key, part):
    tables = hierarchy_tables(key)
    return tables[1]


def draw_lower(key, part):
    tables = hierarchy_tables(key)
    return tables[2]


def draw_ham(key, part):
    key = jax.random.fold_in(key, 21)
    sym_key, anti_key, diag_key = jax.random.split(key, 3)
    sym_src = jax.random.normal(sym_key, (LEVELS, LEVELS), jnp.float32)
    anti_src = jax.random.normal(anti_key, (LEVELS, LEVELS), jnp.float32)
    scaling = 1.0 / jnp.sqrt(2.0 * LEVELS)
    energies = jax.random.uniform(diag_key, (LEVELS,), jnp.float32, -1.0, 1.0)
    ham_real = (sym_src + sym_src.T) * scaling + jnp.diag(energies)
    ham_imag = (anti_src - anti_src.T) * scaling
    return jnp.stack([ham_real, ham_imag]).astype(jnp.bfloat16)


def draw_couple(key, part):
    key = jax.random.fold_in(key, 31)
    source = jax.random.normal(key, (MODES, LEVELS, LEVELS), jnp.float32)
    scaling = 1.0 / jnp.sqrt(2.0 * LEVELS)
    return ((source + jnp.transpose(source, (0, 2, 1))) * scaling).astype(jnp.bfloat16)


def block_levels(key, extent, pieces, low, largest):
    level, own = 1.0, jax.random.fold_in(key, 6)
    for dim, blocks in pieces:
        steps = jnp.exp(jax.random.uniform(jax.random.fold_in(own, dim), (blocks,), jnp.float32, low / len(pieces), largest / len(pieces)))
        level = level * jnp.repeat(steps, extent[dim] // blocks).reshape([-1 if axis == dim else 1 for axis in range(len(extent))])
    return level


def noise(stream_key, dims, scale, bound, cuts=(), kind=jnp.bfloat16):
    entries = jax.random.normal(stream_key, dims, jnp.float32) * scale
    if len(cuts) > 0:
        entries = block_levels(stream_key, dims, cuts, -0.22, 0.18) * entries
    return jnp.clip(entries, min=-bound, max=bound).astype(kind)


def setup_inputs(seed: int = 0) -> dict:
    key_of = jax.random.split(jax.random.key(seed), 11)
    rho_real = noise(key_of[0], (AUX, LEVELS, LEVELS), 1.0, 6.0, ((0, 256), (1, 2)), jnp.float32)
    rho_imag = noise(key_of[1], (AUX, LEVELS, LEVELS), 1.0, 6.0, ((0, 256), (1, 2)), jnp.float32)
    ham = draw_ham(jax.random.fold_in(key_of[10], 71), 0)
    couple = draw_couple(jax.random.fold_in(key_of[10], 71), 0)
    rates = jnp.clip(jnp.exp(jax.random.uniform(key_of[4], (MODES,), jnp.float32, math.log(0.1), math.log(2.0))), 0.1, 2.0)
    coeff_real = jnp.clip(jax.random.uniform(key_of[5], (MODES,), jnp.float32, 0.2, 1.5), 0.2, 1.5)
    coeff_imag = jnp.clip(jax.random.uniform(key_of[6], (MODES,), jnp.float32, -1.0, 1.0), -1.0, 1.0)
    occupation = draw_occupation(jax.random.fold_in(key_of[10], 71), 0)
    upper = draw_upper(jax.random.fold_in(key_of[10], 71), 0)
    lower = draw_lower(jax.random.fold_in(key_of[10], 71), 0)
    return {"rho_real": rho_real, "rho_imag": rho_imag, "ham": ham, "couple": couple, "rates": rates, "coeff_real": coeff_real, "coeff_imag": coeff_imag, "occupation": occupation, "upper": upper, "lower": lower}


step_size = 0.1


def to_bfloat(values):
    return lax.optimization_barrier(values.astype(jnp.bfloat16)).astype(jnp.float32)


def left_apply(matrix, batched):
    return jnp.einsum('ij,ajk->aik', matrix, batched)


def right_apply(batched, matrix):
    return jnp.einsum('aij,jk->aik', batched, matrix)


def derivative(states, ham_real, ham_imag, couple_float, rates, coeff_real, coeff_imag, occupation, upper, lower):
    rounded = to_bfloat(states)
    part_real = rounded[0]
    part_imag = rounded[1]
    prod_real = left_apply(ham_real, part_real) - left_apply(ham_imag, part_imag)
    prod_imag = left_apply(ham_real, part_imag) + left_apply(ham_imag, part_real)
    back_real = right_apply(part_real, ham_real) - right_apply(part_imag, ham_imag)
    back_imag = right_apply(part_real, ham_imag) + right_apply(part_imag, ham_real)
    comm_real = prod_real - back_real
    comm_imag = prod_imag - back_imag
    occ_float = occupation.astype(jnp.float32)
    decay_rate = jnp.dot(occ_float, rates)
    running = jnp.stack([comm_imag, -comm_real]) - decay_rate[None, :, None, None] * states

    def per_mode(mode_pos, running_sum):
        matrix = couple_float[mode_pos]
        left_real = left_apply(matrix, part_real)
        left_imag = left_apply(matrix, part_imag)
        right_real = right_apply(part_real, matrix)
        right_imag = right_apply(part_imag, matrix)
        differ_real = left_real - right_real
        differ_imag = left_imag - right_imag
        summed_real = left_real + right_real
        summed_imag = left_imag + right_imag
        upward = to_bfloat(jnp.stack([differ_imag, -differ_real]))
        coeff_a = coeff_real[mode_pos]
        coeff_b = coeff_imag[mode_pos]
        cross_real = coeff_a * differ_real - coeff_b * summed_imag
        cross_imag = coeff_a * differ_imag + coeff_b * summed_real
        downward = to_bfloat(jnp.stack([cross_imag, -cross_real]))
        up_index = upper[:, mode_pos]
        up_valid = (up_index >= 0).astype(jnp.float32)
        up_safe = jnp.maximum(up_index, 0).astype(jnp.int32)
        down_index = lower[:, mode_pos]
        down_weight = (down_index >= 0).astype(jnp.float32) * occ_float[:, mode_pos]
        down_safe = jnp.maximum(down_index, 0).astype(jnp.int32)
        running_sum = running_sum + jnp.take(upward, up_safe, axis=1) * up_valid[None, :, None, None]
        running_sum = running_sum + jnp.take(downward, down_safe, axis=1) * down_weight[None, :, None, None]
        return running_sum

    return lax.fori_loop(0, MODES, per_mode, running)


def reference(rho_real, rho_imag, ham, couple, rates, coeff_real, coeff_imag, occupation, upper, lower):
    ham_float = ham.astype(jnp.float32)
    couple_float = couple.astype(jnp.float32)
    states = jnp.stack([rho_real, rho_imag])
    first_slope = derivative(states, ham_float[0], ham_float[1], couple_float, rates, coeff_real, coeff_imag, occupation, upper, lower)
    middle = states + step_size * first_slope
    second = derivative(middle, ham_float[0], ham_float[1], couple_float, rates, coeff_real, coeff_imag, occupation, upper, lower)
    result = states + (0.5 * step_size) * (first_slope + second)
    return result[0], result[1]
```

```python
import jax
import jax.numpy as jnp
from jax import lax
from jax.experimental import pallas as pl
from jax.experimental.pallas import tpu as pltpu
from jax.sharding import PartitionSpec as P

step_size = 0.1
half_step = 0.5 * step_size
float32 = jnp.float32
bfloat16 = jnp.bfloat16


def swapped(value, axis, distance):
    pairs = [(source, source ^ distance) for source in range(lax.axis_size(axis))]
    return lax.ppermute(value, axis, pairs)


def forwarded(value, axis, stride):
    ring = 4 * stride
    pairs = []
    for source in range(lax.axis_size(axis)):
        base, place = source - source % ring, source % ring
        shift = stride if source & stride else -stride
        pairs.append((source, base + (place + shift) % ring))
    return lax.ppermute(value, axis, pairs)


def dot(left, right):
    return jnp.dot(left, right, preferred_element_type=float32)


def add_term(total, matrix, real, imag, weight_a, weight_b):
    left_real = dot(matrix, real)
    right_real = dot(real, matrix)
    left_imag = dot(matrix, imag)
    right_imag = dot(imag, matrix)
    total[0] += weight_b * (left_real + right_real) + weight_a * (left_imag - right_imag)
    total[1] += weight_b * (left_imag + right_imag) - weight_a * (left_real - right_real)


def add_commutator(total, ham_ref, real, imag):
    ham_real, ham_imag = ham_ref[0], ham_ref[1]
    total[0] += dot(ham_real, imag) + dot(ham_imag, real) - dot(real, ham_imag) - dot(imag, ham_real)
    total[1] += dot(ham_imag, imag) - dot(ham_real, real) + dot(real, ham_real) - dot(imag, ham_imag)


def rows_of(first):
    return pl.ds(pl.multiple_of(first * 128, 128), 128)


def early_kernel(bits, with_prior, index_ref, coef_ref, ham_ref, couple_ref, own_ref, *refs):
    if with_prior:
        prior_ref, *refs = refs
    partner_refs, total = refs[:-1], refs[-1]
    if with_prior:
        total[...] = coef_ref[2, 1] * prior_ref[...]
    else:
        total[...] = jnp.zeros_like(total)
    add_commutator(total, ham_ref, own_ref[0], own_ref[1])
    for bit, ref in zip(bits, partner_refs, strict=True):
        matrix = couple_ref[index_ref[1 + bit]]
        add_term(total, matrix, ref[0], ref[1], coef_ref[0, bit], coef_ref[1, bit])


def gather_rows(whole, index_ref, near_ref, far_ref):
    near = index_ref[0]
    whole[:, rows_of(near), :] = near_ref[...]
    whole[:, rows_of(1 - near), :] = far_ref[...]


def late_total(bits, index_ref, coef_ref, couple_ref, total_ref, pairs, whole, total):
    total[...] = total_ref[...]
    for bit, (near_ref, far_ref) in zip(bits, pairs, strict=True):
        gather_rows(whole, index_ref, near_ref, far_ref)
        matrix = couple_ref[index_ref[1 + bit]]
        add_term(total, matrix, whole[0], whole[1], coef_ref[0, bit], coef_ref[1, bit])


def middle_kernel(bits, index_ref, coef_ref, couple_ref, own_ref, total_ref, *refs):
    count = 2 * len(bits)
    pairs = list(zip(refs[0:count:2], refs[1:count:2]))
    slope_ref, middle_ref, near_ref, far_ref, whole = refs[count:]
    late_total(bits, index_ref, coef_ref, couple_ref, total_ref, pairs, whole, slope_ref)
    near = index_ref[0]
    middle = coef_ref[2, 0] * own_ref[...].astype(float32) + step_size * slope_ref[...]
    middle_ref[...] = middle.astype(bfloat16)
    near_ref[...] = middle_ref[:, rows_of(near), :]
    far_ref[...] = middle_ref[:, rows_of(1 - near), :]


def last_kernel(bits, index_ref, coef_ref, couple_ref, total_ref, *refs):
    count = 2 * len(bits)
    pairs = list(zip(refs[0:count:2], refs[1:count:2]))
    near_ref, far_ref, whole, total = refs[count:]
    late_total(bits, index_ref, coef_ref, couple_ref, total_ref, pairs, whole, total)
    near = index_ref[0]
    near_ref[...] = half_step * total[:, rows_of(near), :]
    far_ref[...] = (half_step * total[:, rows_of(1 - near), :]).astype(bfloat16)


in_vmem = pl.BlockSpec(memory_space=pltpu.VMEM)
in_smem = pl.BlockSpec(memory_space=pltpu.SMEM)


def call(body, terms, outs, scratch, *operands):
    specs = [in_smem, in_smem] + [in_vmem] * (len(operands) - 2)
    moved = sum(x.size * x.dtype.itemsize for x in operands) + sum(x.size * x.dtype.itemsize for x in outs)
    return pl.pallas_call(
        body,
        out_shape=outs,
        in_specs=specs,
        out_specs=[in_vmem] * len(outs),
        scratch_shapes=scratch,
        cost_estimate=pl.CostEstimate(flops=terms * 8 * 256**3, bytes_accessed=moved, transcendentals=0),
        compiler_params=pltpu.CompilerParams(vmem_limit_bytes=24 * 2**20),
    )(*operands)


def shaped(kind, *dims):
    return jax.ShapeDtypeStruct(dims, kind)


def local(rho_real, rho_imag, ham, couple, rates, coeff_real, coeff_imag, occupation, upper, lower):
    rep = lax.axis_index("rep")
    hier = lax.axis_index("hier")
    rows, levels = rho_real.shape[1:]
    bit_count = lax.axis_size("hier").bit_length()
    x_dist = lax.axis_size("hier") // 2

    own_index = 2 * hier + rep
    occ_float = occupation.astype(float32)
    decay = jnp.sum(occ_float * rates[None, :], axis=1)
    pick = lambda table: jnp.where(rep == 0, table[0], table[1])
    own_occ, own_up, own_low, own_decay = pick(occ_float), pick(upper), pick(lower), pick(decay)
    partner = jnp.bitwise_xor(own_index, jnp.left_shift(1, jnp.arange(bit_count, dtype=jnp.int32)))
    is_above = own_up[None, :] == partner[:, None]
    is_below = own_low[None, :] == partner[:, None]
    mode_range = jnp.arange(couple.shape[0], dtype=jnp.int32)
    modes = jnp.sum(jnp.where(is_above | is_below, mode_range[None, :], 0), axis=1)
    weight_a = jnp.sum(jnp.where(is_above, 1.0, jnp.where(is_below, (own_occ * coeff_real)[None, :], 0.0)), axis=1)
    weight_b = jnp.sum(jnp.where(is_below, (own_occ * coeff_imag)[None, :], 0.0), axis=1)
    keep = 1.0 - step_size * own_decay
    index = jnp.concatenate([rep[None], modes]).astype(jnp.int32)
    keeps = jnp.where(jnp.arange(bit_count) < 2, keep, 0.0)
    coef = jnp.stack([weight_a, weight_b, keeps]).astype(float32)

    whole = shaped(bfloat16, 2, levels, levels)
    slope = shaped(float32, 2, levels, levels)
    half = shaped(bfloat16, 2, rows, levels)
    half_float = shaped(float32, 2, rows, levels)

    def exchange(near, far, full):
        z4_near = swapped(near, "hier", 32)
        z4_far = swapped(far, "hier", 32)
        z2 = swapped(full, "hier", 16)
        z1 = swapped(full, "hier", 8)
        z8_near = forwarded(z4_near, "hier", 32)
        y2 = swapped(full, "hier", 4)
        y1 = swapped(full, "hier", 2)
        z8_far = forwarded(z4_far, "hier", 32)
        x1 = swapped(full, "hier", x_dist)
        x2 = swapped(full, "rep", 1)
        core = swapped(full, "hier", 1)
        return (x2, core, y1, y2, z1, z2, x1), (z4_near, z4_far, z8_near, z8_far)

    early_bits = (0, 1, 2, 3, 4, 5, 8)
    late_bits = (6, 7)

    rounded = jnp.stack([rho_real, rho_imag]).astype(bfloat16)
    near = jnp.where(rep == 0, rounded[:, 0], rounded[:, 1])
    away = jnp.where(rep == 0, rounded[:, 1], rounded[:, 0])
    far = swapped(away, "rep", 1)
    full = jnp.where(rep == 0, jnp.concatenate([near, far], axis=1), jnp.concatenate([far, near], axis=1))

    early, late = exchange(near, far, full)
    total = call(
        lambda *refs: early_kernel(early_bits, False, *refs), 2 + len(early_bits), [slope], [],
        index, coef, ham, couple, full, *early,
    )[0]
    first, middle, near, far = call(
        lambda *refs: middle_kernel(late_bits, *refs), len(late_bits), [slope, whole, half, half],
        [pltpu.VMEM((2, levels, levels), bfloat16)],
        index, coef, couple, full, total, *late,
    )

    early, late = exchange(near, far, middle)
    total = call(
        lambda *refs: early_kernel(early_bits, True, *refs), 2 + len(early_bits), [slope], [],
        index, coef, ham, couple, middle, first, *early,
    )[0]
    near, away = call(
        lambda *refs: last_kernel(late_bits, *refs), len(late_bits), [half_float, half],
        [pltpu.VMEM((2, levels, levels), bfloat16), pltpu.VMEM((2, levels, levels), float32)],
        index, coef, couple, total, *late,
    )
    far = swapped(away, "rep", 1).astype(float32)
    stay = 1.0 - step_size * decay + (0.5 * step_size * step_size) * decay * decay
    is_own = (jnp.arange(2) == rep)[:, None, None]
    outs = []
    for part, state in enumerate((rho_real, rho_imag)):
        change = jnp.where(is_own, near[part][None], far[part][None])
        outs.append(stay[:, None, None] * state + change)
    return tuple(outs)


def solution(mesh):
    placed = (
        P("hier", "rep", None),
        P("hier", "rep", None),
        P(),
        P(),
        P(),
        P(),
        P(),
        P("hier", None),
        P("hier", None),
        P("hier", None),
    )
    return jax.shard_map(
        local,
        mesh=mesh,
        in_specs=placed,
        out_specs=(P("hier", "rep", None), P("hier", "rep", None)),
        check_vma=False,
    )
```

```python
import functools

import jax
import jax.numpy as jnp
from jax import lax
from jax.experimental import pallas as pl
from jax.experimental.pallas import tpu as pltpu
from jax.sharding import Mesh, PartitionSpec as P

step_size = 0.1
half_step = 0.5 * step_size
float32 = jnp.float32
bfloat16 = jnp.bfloat16

hier = ("x_lo", "z", "y", "core")
hier_sizes = (2, 16, 4, 2)


def swapped(value, axis, distance):
    pairs = [(source, source ^ distance) for source in range(lax.axis_size(axis))]
    return lax.ppermute(value, axis, pairs)


def across(value, near_core, far_core):
    ring, cores = lax.axis_size("z"), lax.axis_size("core")
    pairs = []
    for source in range(ring):
        for core, target in enumerate((near_core, far_core)):
            if target is not None:
                pairs.append((source * cores + core, target(source) % ring * cores + core))
    return lax.ppermute(value, ("z", "core"), pairs)


def inward(source):
    return source ^ 4


def outward(source):
    return source - 4 if not source & 4 else source + 4


def after(value, *earlier):
    return lax.optimization_barrier((value, *earlier))[0]


def dot(left, right):
    return jnp.dot(left, right, preferred_element_type=float32)


def add_term(total, matrix, real, imag, weight_a, weight_b):
    left_real = dot(matrix, real)
    right_real = dot(real, matrix)
    left_imag = dot(matrix, imag)
    right_imag = dot(imag, matrix)
    total[0] += weight_b * (left_real + right_real) + weight_a * (left_imag - right_imag)
    total[1] += weight_b * (left_imag + right_imag) - weight_a * (left_real - right_real)


def add_commutator(total, ham_ref, real, imag):
    ham_real, ham_imag = ham_ref[0], ham_ref[1]
    total[0] += dot(ham_real, imag) + dot(ham_imag, real) - dot(real, ham_imag) - dot(imag, ham_real)
    total[1] += dot(ham_imag, imag) - dot(ham_real, real) + dot(real, ham_real) - dot(imag, ham_imag)


def rows_of(first, count):
    return pl.ds(pl.multiple_of(first * count, count), count)


def add_bits(total, parts, index_ref, coef_ref, couple_ref, refs, whole):
    for bit, places in parts:
        source = refs[places[0]]
        if len(places) == 2:
            other = refs[places[1]]
            is_first = index_ref[19] == 0
            whole[...] = jnp.where(is_first, source[...], other[...])
            source = whole
        elif len(source.shape) == 4:
            source = source.at[index_ref[10 + bit]]
        matrix = couple_ref[index_ref[1 + bit]]
        add_term(total, matrix, source[0], source[1], coef_ref[0, bit], coef_ref[1, bit])


def early_kernel(parts, index_ref, coef_ref, couple_ref, ham_ref, own_ref, *refs, with_prior):
    if with_prior:
        prior_ref, *refs = refs
    *partner_refs, total, whole = refs
    if with_prior:
        total[...] = coef_ref[2, 0] * prior_ref[...]
    else:
        total[...] = jnp.zeros_like(total)
    add_commutator(total, ham_ref, own_ref[0], own_ref[1])
    add_bits(total, parts, index_ref, coef_ref, couple_ref, partner_refs, whole)


def middle_kernel(parts, index_ref, coef_ref, couple_ref, own_ref, total_ref, *refs):
    *partner_refs, slope_ref, middle_ref, whole = refs
    slope_ref[...] = total_ref[...]
    add_bits(slope_ref, parts, index_ref, coef_ref, couple_ref, partner_refs, whole)
    middle = coef_ref[2, 0] * own_ref[...].astype(float32) + step_size * slope_ref[...]
    middle_ref[...] = middle.astype(bfloat16)


def last_kernel(parts, index_ref, coef_ref, couple_ref, total_ref, *refs):
    *partner_refs, near_ref, far_ref, whole, total = refs
    total[...] = total_ref[...]
    add_bits(total, parts, index_ref, coef_ref, couple_ref, partner_refs, whole)
    near = index_ref[0]
    rows = near_ref.shape[1]
    near_ref[...] = half_step * total[:, rows_of(near, rows), :]
    far_ref[...] = (half_step * total[:, rows_of(1 - near, rows), :]).astype(bfloat16)


in_vmem = pl.BlockSpec(memory_space=pltpu.VMEM)
in_smem = pl.BlockSpec(memory_space=pltpu.SMEM)


def shaped(kind, *dims):
    return jax.ShapeDtypeStruct(dims, kind)


def local(rho_real, rho_imag, ham, couple, rates, coeff_real, coeff_imag, occupation, upper, lower):
    rep = lax.axis_index("rep")
    rows, levels = rho_real.shape[1:]
    bit_count = lax.axis_size(hier).bit_length()

    own_index = 2 * lax.axis_index(hier) + rep
    occ_float = occupation.astype(float32)
    decay = jnp.sum(occ_float * rates[None, :], axis=1)
    pick = lambda table: jnp.where(rep == 0, table[0], table[1])
    own_occ, own_up, own_low, own_decay = pick(occ_float), pick(upper), pick(lower), pick(decay)
    partner = jnp.bitwise_xor(own_index, jnp.left_shift(1, jnp.arange(bit_count, dtype=jnp.int32)))
    is_above = own_up[None, :] == partner[:, None]
    is_below = own_low[None, :] == partner[:, None]
    mode_range = jnp.arange(couple.shape[0], dtype=jnp.int32)
    modes = jnp.sum(jnp.where(is_above | is_below, mode_range[None, :], 0), axis=1)
    weight_a = jnp.sum(jnp.where(is_above, 1.0, jnp.where(is_below, (own_occ * coeff_real)[None, :], 0.0)), axis=1)
    weight_b = jnp.sum(jnp.where(is_below, (own_occ * coeff_imag)[None, :], 0.0), axis=1)
    keep = 1.0 - step_size * own_decay
    x_place = 2 * rep + lax.axis_index("x_lo")
    y_place = lax.axis_index("y")
    places = jnp.array([2, 0, 1, 2, 0, 0, 0, 0, 1], jnp.int32)
    places = jnp.bitwise_xor(jnp.where(jnp.array([i in (0, 8) for i in range(9)]), x_place, y_place), places)
    index = jnp.concatenate([rep[None], modes, places, lax.axis_index("core")[None]]).astype(jnp.int32)
    keeps = jnp.where(jnp.arange(bit_count) < 2, keep, 0.0)
    coef = jnp.stack([weight_a, weight_b, keeps]).astype(float32)

    whole = shaped(bfloat16, 2, levels, levels)
    slope = shaped(float32, 2, levels, levels)
    half = shaped(bfloat16, 2, rows, levels)
    half_float = shaped(float32, 2, rows, levels)

    def exchange(full):
        first = across(full, inward, outward)
        z2 = swapped(full, "z", 2)
        z1 = swapped(full, "z", 1)
        own = across(full, None, inward)
        second = across(first, outward, inward)
        along_y = lax.all_gather(full, "y", axis=0)
        core = swapped(full, "core", 1)
        x2 = swapped(after(full, z1), "rep", 1)
        x1 = swapped(after(full, z1), "x_lo", 1)
        early = {6: [first, own], 4: [z1], 5: [z2], 1: [core], 8: [x1], 0: [x2], 2: [along_y], 3: [along_y]}
        return early, {7: [second]}

    def call(body, parts, outs, scratch, *operands):
        held = []
        places = []
        for bit, arrays in parts.items():
            for array in arrays:
                if not any(array is other for other in held):
                    held.append(array)
            places.append((bit, tuple(next(i for i, x in enumerate(held) if x is array) for array in arrays)))
        arrays = (index, coef, couple, *operands, *held)
        counts = tuple(places)
        moved = sum(x.size * x.dtype.itemsize for x in (*arrays, *outs))
        return pl.pallas_call(
            lambda *refs: body(counts, *refs),
            out_shape=outs,
            in_specs=[in_smem, in_smem] + [in_vmem] * (len(arrays) - 2),
            out_specs=[in_vmem] * len(outs),
            scratch_shapes=[pltpu.VMEM((2, levels, levels), bfloat16), *scratch],
            cost_estimate=pl.CostEstimate(flops=len(parts) * 8 * levels**3, bytes_accessed=moved, transcendentals=0),
            compiler_params=pltpu.CompilerParams(vmem_limit_bytes=24 * 2**20),
        )(*arrays)

    rounded = jnp.stack([rho_real, rho_imag]).astype(bfloat16)
    near = jnp.where(rep == 0, rounded[:, 0], rounded[:, 1])
    away = jnp.where(rep == 0, rounded[:, 1], rounded[:, 0])
    far = swapped(away, "rep", 1)
    full = jnp.where(rep == 0, jnp.concatenate([near, far], axis=1), jnp.concatenate([far, near], axis=1))

    early, late = exchange(full)
    (total,) = call(functools.partial(early_kernel, with_prior=False), early, [slope], [], ham, full)
    first, middle = call(middle_kernel, late, [slope, whole], [], full, total)

    early, late = exchange(middle)
    (total,) = call(functools.partial(early_kernel, with_prior=True), early, [slope], [], ham, middle, first)
    near, away = call(last_kernel, late, [half_float, half], [pltpu.VMEM((2, levels, levels), float32)], total)
    far = swapped(away, "rep", 1).astype(float32)
    stay = 1.0 - step_size * decay + (0.5 * step_size * step_size) * decay * decay
    is_own = (jnp.arange(2) == rep)[:, None, None]
    outs = []
    for part, state in enumerate((rho_real, rho_imag)):
        change = jnp.where(is_own, near[part][None], far[part][None])
        outs.append(stay[:, None, None] * state + change)
    return tuple(outs)


def solution(mesh):
    axes = Mesh(mesh.devices.reshape(*hier_sizes, mesh.shape["rep"]), (*hier, "rep"))
    placed = (
        P(hier, "rep", None),
        P(hier, "rep", None),
        P(),
        P(),
        P(),
        P(),
        P(),
        P(hier, None),
        P(hier, None),
        P(hier, None),
    )
    return jax.shard_map(
        local,
        mesh=axes,
        in_specs=placed,
        out_specs=(P(hier, "rep", None), P(hier, "rep", None)),
        check_vma=False,
    )
```

```python
import functools

import jax
import jax.numpy as jnp
from jax import lax
from jax.experimental import pallas as pl
from jax.experimental.pallas import tpu as pltpu
from jax.sharding import Mesh, PartitionSpec as P

step_size = 0.1
half_step = 0.5 * step_size
float32 = jnp.float32
bfloat16 = jnp.bfloat16

hier = ("x_lo", "z", "y", "core")
hier_sizes = (2, 16, 4, 2)


def swapped(value, axis, distance):
    pairs = [(source, source ^ distance) for source in range(lax.axis_size(axis))]
    return lax.ppermute(value, axis, pairs)


def across(value, near_core, far_core):
    ring, cores = lax.axis_size("z"), lax.axis_size("core")
    pairs = []
    for source in range(ring):
        for core, target in enumerate((near_core, far_core)):
            if target is not None:
                pairs.append((source * cores + core, target(source) % ring * cores + core))
    return lax.ppermute(value, ("z", "core"), pairs)


def inward(source):
    return source ^ 4


def opposite(source):
    return source ^ 8


def outward(source):
    return source - 4 if not source & 4 else source + 4


def after(value, *earlier):
    return lax.optimization_barrier((value, *earlier))[0]


def dot(left, right):
    return jnp.dot(left, right, preferred_element_type=float32)


def add_term(total, matrix, real, imag, weight_a, weight_b):
    left_real = dot(matrix, real)
    right_real = dot(real, matrix)
    left_imag = dot(matrix, imag)
    right_imag = dot(imag, matrix)
    total[0] += weight_b * (left_real + right_real) + weight_a * (left_imag - right_imag)
    total[1] += weight_b * (left_imag + right_imag) - weight_a * (left_real - right_real)


def add_commutator(total, ham_ref, real, imag):
    ham_real, ham_imag = ham_ref[0], ham_ref[1]
    total[0] += dot(ham_real, imag) + dot(ham_imag, real) - dot(real, ham_imag) - dot(imag, ham_real)
    total[1] += dot(ham_imag, imag) - dot(ham_real, real) + dot(real, ham_real) - dot(imag, ham_imag)


def rows_of(first, count):
    return pl.ds(pl.multiple_of(first * count, count), count)


def add_bits(total, parts, index_ref, coef_ref, couple_ref, refs, whole):
    for bit, places in parts:
        source = refs[places[0]]
        if len(places) == 2:
            whole[...] = jnp.where(index_ref[10] == 0, source[...], refs[places[1]][...])
            source = whole
        matrix = couple_ref[index_ref[1 + bit]]
        add_term(total, matrix, source[0], source[1], coef_ref[0, bit], coef_ref[1, bit])


def early_kernel(parts, index_ref, coef_ref, couple_ref, ham_ref, own_ref, *refs, with_prior):
    if with_prior:
        prior_ref, *refs = refs
    *partner_refs, total, whole = refs
    if with_prior:
        total[...] = coef_ref[2, 0] * prior_ref[...]
    else:
        total[...] = jnp.zeros_like(total)
    add_commutator(total, ham_ref, own_ref[0], own_ref[1])
    add_bits(total, parts, index_ref, coef_ref, couple_ref, partner_refs, whole)


def middle_kernel(parts, index_ref, coef_ref, couple_ref, own_ref, total_ref, *refs):
    *partner_refs, slope_ref, middle_ref, whole = refs
    slope_ref[...] = total_ref[...]
    add_bits(slope_ref, parts, index_ref, coef_ref, couple_ref, partner_refs, whole)
    middle = coef_ref[2, 0] * own_ref[...].astype(float32) + step_size * slope_ref[...]
    middle_ref[...] = middle.astype(bfloat16)


def last_kernel(parts, index_ref, coef_ref, couple_ref, total_ref, *refs):
    *partner_refs, near_ref, far_ref, whole, total = refs
    total[...] = total_ref[...]
    add_bits(total, parts, index_ref, coef_ref, couple_ref, partner_refs, whole)
    near = index_ref[0]
    rows = near_ref.shape[1]
    near_ref[...] = half_step * total[:, rows_of(near, rows), :]
    far_ref[...] = (half_step * total[:, rows_of(1 - near, rows), :]).astype(bfloat16)


in_vmem = pl.BlockSpec(memory_space=pltpu.VMEM)
in_smem = pl.BlockSpec(memory_space=pltpu.SMEM)


def shaped(kind, *dims):
    return jax.ShapeDtypeStruct(dims, kind)


def local(rho_real, rho_imag, ham, couple, rates, coeff_real, coeff_imag, occupation, upper, lower):
    rep = lax.axis_index("rep")
    rows, levels = rho_real.shape[1:]
    bit_count = lax.axis_size(hier).bit_length()

    own_index = 2 * lax.axis_index(hier) + rep
    occ_float = occupation.astype(float32)
    decay = jnp.sum(occ_float * rates[None, :], axis=1)
    pick = lambda table: jnp.where(rep == 0, table[0], table[1])
    own_occ, own_up, own_low, own_decay = pick(occ_float), pick(upper), pick(lower), pick(decay)
    partner = jnp.bitwise_xor(own_index, jnp.left_shift(1, jnp.arange(bit_count, dtype=jnp.int32)))
    is_above = own_up[None, :] == partner[:, None]
    is_below = own_low[None, :] == partner[:, None]
    mode_range = jnp.arange(couple.shape[0], dtype=jnp.int32)
    modes = jnp.sum(jnp.where(is_above | is_below, mode_range[None, :], 0), axis=1)
    weight_a = jnp.sum(jnp.where(is_above, 1.0, jnp.where(is_below, (own_occ * coeff_real)[None, :], 0.0)), axis=1)
    weight_b = jnp.sum(jnp.where(is_below, (own_occ * coeff_imag)[None, :], 0.0), axis=1)
    keep = 1.0 - step_size * own_decay
    index = jnp.concatenate([rep[None], modes, lax.axis_index("core")[None]]).astype(jnp.int32)
    keeps = jnp.where(jnp.arange(bit_count) < 2, keep, 0.0)
    coef = jnp.stack([weight_a, weight_b, keeps]).astype(float32)

    on_first = lax.axis_index("core") == 0
    whole = shaped(bfloat16, 2, levels, levels)
    slope = shaped(float32, 2, levels, levels)
    half = shaped(bfloat16, 2, rows, levels)
    half_float = shaped(float32, 2, rows, levels)

    def exchange(full):
        z1 = swapped(full, "z", 1)
        core = swapped(full, "core", 1)
        first = across(full, inward, opposite)
        z2 = swapped(full, "z", 2)
        x1 = swapped(full, "x_lo", 1)
        x2 = swapped(after(full, z1), "rep", 1)
        y1 = swapped(after(full, core), "y", 1)
        y2 = swapped(after(full, x1), "y", 2)
        second = across(jnp.where(on_first, first, full), outward, inward)
        early = {4: [z1], 1: [core], 5: [z2], 8: [x1], 0: [x2], 2: [y1], 3: [y2]}
        return early, {6: [first, second], 7: [second, first]}

    def call(body, parts, outs, scratch, *operands):
        held = []
        places = []
        for bit, arrays in parts.items():
            for array in arrays:
                if not any(array is other for other in held):
                    held.append(array)
            places.append((bit, tuple(next(i for i, x in enumerate(held) if x is array) for array in arrays)))
        arrays = (index, coef, couple, *operands, *held)
        counts = tuple(places)
        moved = sum(x.size * x.dtype.itemsize for x in (*arrays, *outs))
        return pl.pallas_call(
            lambda *refs: body(counts, *refs),
            out_shape=outs,
            in_specs=[in_smem, in_smem] + [in_vmem] * (len(arrays) - 2),
            out_specs=[in_vmem] * len(outs),
            scratch_shapes=[pltpu.VMEM((2, levels, levels), bfloat16), *scratch],
            cost_estimate=pl.CostEstimate(flops=len(parts) * 8 * levels**3, bytes_accessed=moved, transcendentals=0),
            compiler_params=pltpu.CompilerParams(vmem_limit_bytes=12 * 2**20),
        )(*arrays)

    rounded = jnp.stack([rho_real, rho_imag]).astype(bfloat16)
    near = jnp.where(rep == 0, rounded[:, 0], rounded[:, 1])
    away = jnp.where(rep == 0, rounded[:, 1], rounded[:, 0])
    far = swapped(away, "rep", 1)
    full = jnp.where(rep == 0, jnp.concatenate([near, far], axis=1), jnp.concatenate([far, near], axis=1))

    early, late = exchange(full)
    (total,) = call(functools.partial(early_kernel, with_prior=False), early, [slope], [], ham, full)
    first, middle = call(middle_kernel, late, [slope, whole], [], full, total)

    early, late = exchange(middle)
    (total,) = call(functools.partial(early_kernel, with_prior=True), early, [slope], [], ham, middle, first)
    near, away = call(last_kernel, late, [half_float, half], [pltpu.VMEM((2, levels, levels), float32)], total)
    far = swapped(away, "rep", 1).astype(float32)
    stay = 1.0 - step_size * decay + (0.5 * step_size * step_size) * decay * decay
    is_own = (jnp.arange(2) == rep)[:, None, None]
    outs = []
    for part, state in enumerate((rho_real, rho_imag)):
        change = jnp.where(is_own, near[part][None], far[part][None])
        outs.append(stay[:, None, None] * state + change)
    return tuple(outs)


def solution(mesh):
    axes = Mesh(mesh.devices.reshape(*hier_sizes, mesh.shape["rep"]), (*hier, "rep"))
    placed = (
        P(hier, "rep", None),
        P(hier, "rep", None),
        P(),
        P(),
        P(),
        P(),
        P(),
        P(hier, None),
        P(hier, None),
        P(hier, None),
    )
    return jax.shard_map(
        local,
        mesh=axes,
        in_specs=placed,
        out_specs=(P(hier, "rep", None), P(hier, "rep", None)),
        check_vma=False,
    )
```

```python
import functools

import jax
import jax.numpy as jnp
from jax import lax
from jax.experimental import pallas as pl
from jax.experimental.pallas import tpu as pltpu
from jax.sharding import Mesh, PartitionSpec as P

step_size = 0.1
half_step = 0.5 * step_size
float32 = jnp.float32
bfloat16 = jnp.bfloat16

hier = ("x_lo", "z", "y", "core")
hier_sizes = (2, 16, 4, 2)


def swapped(value, axis, distance):
    pairs = [(source, source ^ distance) for source in range(lax.axis_size(axis))]
    return lax.ppermute(value, axis, pairs)


def across(value, near_core, far_core):
    ring, cores = lax.axis_size("z"), lax.axis_size("core")
    pairs = []
    for source in range(ring):
        for core, target in enumerate((near_core, far_core)):
            if target is not None:
                pairs.append((source * cores + core, target(source) % ring * cores + core))
    return lax.ppermute(value, ("z", "core"), pairs)


def inward(source):
    return source ^ 4


def opposite(source):
    return source ^ 8


def outward(source):
    return source - 4 if not source & 4 else source + 4


def after(value, *earlier):
    return lax.optimization_barrier((value, *earlier))[0]


def dot(left, right):
    return jnp.dot(left, right, preferred_element_type=float32)


def add_term(total, matrix, real, imag, weight_a, weight_b):
    left_real = dot(matrix, real)
    right_real = dot(real, matrix)
    left_imag = dot(matrix, imag)
    right_imag = dot(imag, matrix)
    total[0] += weight_b * (left_real + right_real) + weight_a * (left_imag - right_imag)
    total[1] += weight_b * (left_imag + right_imag) - weight_a * (left_real - right_real)


def add_commutator(total, ham_ref, real, imag):
    ham_real, ham_imag = ham_ref[0], ham_ref[1]
    total[0] += dot(ham_real, imag) + dot(ham_imag, real) - dot(real, ham_imag) - dot(imag, ham_real)
    total[1] += dot(ham_imag, imag) - dot(ham_real, real) + dot(real, ham_real) - dot(imag, ham_imag)


def rows_of(first, count):
    return pl.ds(pl.multiple_of(first * count, count), count)


def add_bits(total, parts, index_ref, coef_ref, couple_ref, refs, whole):
    for bit, places in parts:
        source = refs[places[0]]
        if len(places) == 2:
            whole[...] = jnp.where(index_ref[10] == 0, source[...], refs[places[1]][...])
            source = whole
        matrix = couple_ref[index_ref[1 + bit]]
        add_term(total, matrix, source[0], source[1], coef_ref[0, bit], coef_ref[1, bit])


def early_kernel(parts, index_ref, coef_ref, couple_ref, ham_ref, own_ref, *refs, with_prior):
    if with_prior:
        prior_ref, *refs = refs
    *partner_refs, total, whole = refs
    if with_prior:
        total[...] = coef_ref[2, 0] * prior_ref[...]
    else:
        total[...] = jnp.zeros_like(total)
    add_commutator(total, ham_ref, own_ref[0], own_ref[1])
    add_bits(total, parts, index_ref, coef_ref, couple_ref, partner_refs, whole)


def add_kernel(parts, index_ref, coef_ref, couple_ref, total_ref, *refs):
    *partner_refs, out_ref, whole = refs
    out_ref[...] = total_ref[...]
    add_bits(out_ref, parts, index_ref, coef_ref, couple_ref, partner_refs, whole)


def middle_kernel(parts, index_ref, coef_ref, couple_ref, own_ref, total_ref, *refs):
    *partner_refs, slope_ref, middle_ref, whole = refs
    slope_ref[...] = total_ref[...]
    add_bits(slope_ref, parts, index_ref, coef_ref, couple_ref, partner_refs, whole)
    middle = coef_ref[2, 0] * own_ref[...].astype(float32) + step_size * slope_ref[...]
    middle_ref[...] = middle.astype(bfloat16)


def last_kernel(parts, index_ref, coef_ref, couple_ref, total_ref, *refs):
    *partner_refs, near_ref, far_ref, whole, total = refs
    total[...] = total_ref[...]
    add_bits(total, parts, index_ref, coef_ref, couple_ref, partner_refs, whole)
    near = index_ref[0]
    rows = near_ref.shape[1]
    near_ref[...] = half_step * total[:, rows_of(near, rows), :]
    far_ref[...] = (half_step * total[:, rows_of(1 - near, rows), :]).astype(bfloat16)


in_vmem = pl.BlockSpec(memory_space=pltpu.VMEM)
in_smem = pl.BlockSpec(memory_space=pltpu.SMEM)


def shaped(kind, *dims):
    return jax.ShapeDtypeStruct(dims, kind)


def local(rho_real, rho_imag, ham, couple, rates, coeff_real, coeff_imag, occupation, upper, lower):
    rep = lax.axis_index("rep")
    rows, levels = rho_real.shape[1:]
    bit_count = lax.axis_size(hier).bit_length()

    own_index = 2 * lax.axis_index(hier) + rep
    occ_float = occupation.astype(float32)
    decay = jnp.sum(occ_float * rates[None, :], axis=1)
    pick = lambda table: jnp.where(rep == 0, table[0], table[1])
    own_occ, own_up, own_low, own_decay = pick(occ_float), pick(upper), pick(lower), pick(decay)
    partner = jnp.bitwise_xor(own_index, jnp.left_shift(1, jnp.arange(bit_count, dtype=jnp.int32)))
    is_above = own_up[None, :] == partner[:, None]
    is_below = own_low[None, :] == partner[:, None]
    mode_range = jnp.arange(couple.shape[0], dtype=jnp.int32)
    modes = jnp.sum(jnp.where(is_above | is_below, mode_range[None, :], 0), axis=1)
    weight_a = jnp.sum(jnp.where(is_above, 1.0, jnp.where(is_below, (own_occ * coeff_real)[None, :], 0.0)), axis=1)
    weight_b = jnp.sum(jnp.where(is_below, (own_occ * coeff_imag)[None, :], 0.0), axis=1)
    keep = 1.0 - step_size * own_decay
    index = jnp.concatenate([rep[None], modes, lax.axis_index("core")[None]]).astype(jnp.int32)
    keeps = jnp.where(jnp.arange(bit_count) < 2, keep, 0.0)
    coef = jnp.stack([weight_a, weight_b, keeps]).astype(float32)

    on_first = lax.axis_index("core") == 0
    whole = shaped(bfloat16, 2, levels, levels)
    slope = shaped(float32, 2, levels, levels)
    half = shaped(bfloat16, 2, rows, levels)
    half_float = shaped(float32, 2, rows, levels)

    def exchange(full):
        z2 = swapped(full, "z", 2)
        first = across(full, inward, opposite)
        z1 = swapped(full, "z", 1)
        core = swapped(full, "core", 1)
        x1 = swapped(full, "x_lo", 1)
        x2 = swapped(after(full, z2), "rep", 1)
        y1 = swapped(after(full, first, z1), "y", 1)
        y2 = swapped(after(full, first, core), "y", 2)
        second = across(jnp.where(on_first, first, full), outward, inward)
        return {5: [z2], 4: [z1], 1: [core], 8: [x1], 0: [x2]}, {6: [first, second], 7: [second, first]}, {2: [y1], 3: [y2]}

    def call(body, parts, outs, scratch, *operands):
        held = []
        places = []
        for bit, arrays in parts.items():
            for array in arrays:
                if not any(array is other for other in held):
                    held.append(array)
            places.append((bit, tuple(next(i for i, x in enumerate(held) if x is array) for array in arrays)))
        arrays = (index, coef, couple, *operands, *held)
        counts = tuple(places)
        moved = sum(x.size * x.dtype.itemsize for x in (*arrays, *outs))
        return pl.pallas_call(
            lambda *refs: body(counts, *refs),
            out_shape=outs,
            in_specs=[in_smem, in_smem] + [in_vmem] * (len(arrays) - 2),
            out_specs=[in_vmem] * len(outs),
            scratch_shapes=[pltpu.VMEM((2, levels, levels), bfloat16), *scratch],
            cost_estimate=pl.CostEstimate(flops=len(parts) * 8 * levels**3, bytes_accessed=moved, transcendentals=0),
            compiler_params=pltpu.CompilerParams(vmem_limit_bytes=12 * 2**20),
        )(*arrays)

    rounded = jnp.stack([rho_real, rho_imag]).astype(bfloat16)
    near = jnp.where(rep == 0, rounded[:, 0], rounded[:, 1])
    away = jnp.where(rep == 0, rounded[:, 1], rounded[:, 0])
    far = swapped(away, "rep", 1)
    full = jnp.where(rep == 0, jnp.concatenate([near, far], axis=1), jnp.concatenate([far, near], axis=1))

    early, inner, late = exchange(full)
    (total,) = call(functools.partial(early_kernel, with_prior=False), early, [slope], [], ham, full)
    (total,) = call(add_kernel, inner, [slope], [], total)
    first, middle = call(middle_kernel, late, [slope, whole], [], full, total)

    early, inner, late = exchange(middle)
    (total,) = call(functools.partial(early_kernel, with_prior=True), early, [slope], [], ham, middle, first)
    (total,) = call(add_kernel, inner, [slope], [], total)
    near, away = call(last_kernel, late, [half_float, half], [pltpu.VMEM((2, levels, levels), float32)], total)
    far = swapped(away, "rep", 1).astype(float32)
    stay = 1.0 - step_size * decay + (0.5 * step_size * step_size) * decay * decay
    is_own = (jnp.arange(2) == rep)[:, None, None]
    outs = []
    for part, state in enumerate((rho_real, rho_imag)):
        change = jnp.where(is_own, near[part][None], far[part][None])
        outs.append(stay[:, None, None] * state + change)
    return tuple(outs)


def solution(mesh):
    axes = Mesh(mesh.devices.reshape(*hier_sizes, mesh.shape["rep"]), (*hier, "rep"))
    placed = (
        P(hier, "rep", None),
        P(hier, "rep", None),
        P(),
        P(),
        P(),
        P(),
        P(),
        P(hier, None),
        P(hier, None),
        P(hier, None),
    )
    return jax.shard_map(
        local,
        mesh=axes,
        in_specs=placed,
        out_specs=(P(hier, "rep", None), P(hier, "rep", None)),
        check_vma=False,
    )
```

```python
import functools

import jax
import jax.numpy as jnp
from jax import lax
from jax.experimental import pallas as pl
from jax.experimental.pallas import tpu as pltpu
from jax.sharding import Mesh, PartitionSpec as P

step_size = 0.1
half_step = 0.5 * step_size
float32 = jnp.float32
bfloat16 = jnp.bfloat16

hier = ("x_lo", "z", "y", "core")
hier_sizes = (2, 16, 4, 2)


def swapped(value, axis, distance):
    pairs = [(source, source ^ distance) for source in range(lax.axis_size(axis))]
    return lax.ppermute(value, axis, pairs)


def across(value, near_core, far_core):
    ring, cores = lax.axis_size("z"), lax.axis_size("core")
    pairs = []
    for source in range(ring):
        for core, target in enumerate((near_core, far_core)):
            if target is not None:
                pairs.append((source * cores + core, target(source) % ring * cores + core))
    return lax.ppermute(value, ("z", "core"), pairs)


def inward(source):
    return source ^ 4


def opposite(source):
    return source ^ 8


def outward(source):
    return source - 4 if not source & 4 else source + 4


def after(value, *earlier):
    return lax.optimization_barrier((value, *earlier))[0]


def dot(left, right):
    return jnp.dot(left, right, preferred_element_type=float32)


def add_term(total, matrix, real, imag, weight_a, weight_b):
    left_real = dot(matrix, real)
    right_real = dot(real, matrix)
    left_imag = dot(matrix, imag)
    right_imag = dot(imag, matrix)
    total[0] += weight_b * (left_real + right_real) + weight_a * (left_imag - right_imag)
    total[1] += weight_b * (left_imag + right_imag) - weight_a * (left_real - right_real)


def add_commutator(total, ham_ref, real, imag):
    ham_real, ham_imag = ham_ref[0], ham_ref[1]
    total[0] += dot(ham_real, imag) + dot(ham_imag, real) - dot(real, ham_imag) - dot(imag, ham_real)
    total[1] += dot(ham_imag, imag) - dot(ham_real, real) + dot(real, ham_real) - dot(imag, ham_imag)


def rows_of(first, count):
    return pl.ds(pl.multiple_of(first * count, count), count)


def add_bits(total, parts, index_ref, coef_ref, couple_ref, refs, whole):
    for bit, places in parts:
        source = refs[places[0]]
        if len(places) == 2:
            whole[...] = jnp.where(index_ref[10] == 0, source[...], refs[places[1]][...])
            source = whole
        matrix = couple_ref[index_ref[1 + bit]]
        add_term(total, matrix, source[0], source[1], coef_ref[0, bit], coef_ref[1, bit])


def early_kernel(parts, index_ref, coef_ref, couple_ref, ham_ref, own_ref, *refs, with_prior):
    if with_prior:
        prior_ref, *refs = refs
    *partner_refs, total, whole = refs
    if with_prior:
        total[...] = coef_ref[2, 0] * prior_ref[...]
    else:
        total[...] = jnp.zeros_like(total)
    add_commutator(total, ham_ref, own_ref[0], own_ref[1])
    add_bits(total, parts, index_ref, coef_ref, couple_ref, partner_refs, whole)


def add_kernel(parts, index_ref, coef_ref, couple_ref, total_ref, *refs):
    *partner_refs, out_ref, whole = refs
    out_ref[...] = total_ref[...]
    add_bits(out_ref, parts, index_ref, coef_ref, couple_ref, partner_refs, whole)


def middle_kernel(parts, index_ref, coef_ref, couple_ref, own_ref, total_ref, *refs):
    *partner_refs, slope_ref, middle_ref, whole = refs
    slope_ref[...] = total_ref[...]
    add_bits(slope_ref, parts, index_ref, coef_ref, couple_ref, partner_refs, whole)
    middle = coef_ref[2, 0] * own_ref[...].astype(float32) + step_size * slope_ref[...]
    middle_ref[...] = middle.astype(bfloat16)


def last_kernel(parts, index_ref, coef_ref, couple_ref, total_ref, *refs):
    *partner_refs, near_ref, far_ref, whole, total = refs
    total[...] = total_ref[...]
    add_bits(total, parts, index_ref, coef_ref, couple_ref, partner_refs, whole)
    near = index_ref[0]
    rows = near_ref.shape[1]
    near_ref[...] = half_step * total[:, rows_of(near, rows), :]
    far_ref[...] = (half_step * total[:, rows_of(1 - near, rows), :]).astype(bfloat16)


in_vmem = pl.BlockSpec(memory_space=pltpu.VMEM)
in_smem = pl.BlockSpec(memory_space=pltpu.SMEM)


def shaped(kind, *dims):
    return jax.ShapeDtypeStruct(dims, kind)


def local(rho_real, rho_imag, ham, couple, rates, coeff_real, coeff_imag, occupation, upper, lower):
    rep = lax.axis_index("rep")
    rows, levels = rho_real.shape[1:]
    bit_count = lax.axis_size(hier).bit_length()

    own_index = 2 * lax.axis_index(hier) + rep
    occ_float = occupation.astype(float32)
    decay = jnp.sum(occ_float * rates[None, :], axis=1)
    pick = lambda table: jnp.where(rep == 0, table[0], table[1])
    own_occ, own_up, own_low, own_decay = pick(occ_float), pick(upper), pick(lower), pick(decay)
    partner = jnp.bitwise_xor(own_index, jnp.left_shift(1, jnp.arange(bit_count, dtype=jnp.int32)))
    is_above = own_up[None, :] == partner[:, None]
    is_below = own_low[None, :] == partner[:, None]
    mode_range = jnp.arange(couple.shape[0], dtype=jnp.int32)
    modes = jnp.sum(jnp.where(is_above | is_below, mode_range[None, :], 0), axis=1)
    weight_a = jnp.sum(jnp.where(is_above, 1.0, jnp.where(is_below, (own_occ * coeff_real)[None, :], 0.0)), axis=1)
    weight_b = jnp.sum(jnp.where(is_below, (own_occ * coeff_imag)[None, :], 0.0), axis=1)
    keep = 1.0 - step_size * own_decay
    index = jnp.concatenate([rep[None], modes, lax.axis_index("core")[None]]).astype(jnp.int32)
    keeps = jnp.where(jnp.arange(bit_count) < 2, keep, 0.0)
    coef = jnp.stack([weight_a, weight_b, keeps]).astype(float32)

    on_first = lax.axis_index("core") == 0
    whole = shaped(bfloat16, 2, levels, levels)
    slope = shaped(float32, 2, levels, levels)
    half = shaped(bfloat16, 2, rows, levels)
    half_float = shaped(float32, 2, rows, levels)

    def exchange(full):
        first = across(full, inward, opposite)
        core = swapped(full, "core", 1)
        z2 = swapped(full, "z", 2)
        x2 = swapped(full, "rep", 1)
        y2 = swapped(full, "y", 2)
        z1 = swapped(after(full, first, core), "z", 1)
        x1 = swapped(after(full, first, x2), "x_lo", 1)
        y1 = swapped(after(full, first, z2), "y", 1)
        second = across(jnp.where(on_first, first, full), outward, inward)
        return {1: [core], 5: [z2], 0: [x2], 3: [y2]}, {6: [first, second], 7: [second, first]}, {4: [z1], 8: [x1], 2: [y1]}

    def call(body, parts, outs, scratch, *operands):
        held = []
        places = []
        for bit, arrays in parts.items():
            for array in arrays:
                if not any(array is other for other in held):
                    held.append(array)
            places.append((bit, tuple(next(i for i, x in enumerate(held) if x is array) for array in arrays)))
        arrays = (index, coef, couple, *operands, *held)
        counts = tuple(places)
        moved = sum(x.size * x.dtype.itemsize for x in (*arrays, *outs))
        return pl.pallas_call(
            lambda *refs: body(counts, *refs),
            out_shape=outs,
            in_specs=[in_smem, in_smem] + [in_vmem] * (len(arrays) - 2),
            out_specs=[in_vmem] * len(outs),
            scratch_shapes=[pltpu.VMEM((2, levels, levels), bfloat16), *scratch],
            cost_estimate=pl.CostEstimate(flops=len(parts) * 8 * levels**3, bytes_accessed=moved, transcendentals=0),
            compiler_params=pltpu.CompilerParams(vmem_limit_bytes=12 * 2**20),
        )(*arrays)

    rounded = jnp.stack([rho_real, rho_imag]).astype(bfloat16)
    near = jnp.where(rep == 0, rounded[:, 0], rounded[:, 1])
    away = jnp.where(rep == 0, rounded[:, 1], rounded[:, 0])
    far = swapped(away, "rep", 1)
    full = jnp.where(rep == 0, jnp.concatenate([near, far], axis=1), jnp.concatenate([far, near], axis=1))

    early, inner, late = exchange(full)
    (total,) = call(functools.partial(early_kernel, with_prior=False), early, [slope], [], ham, full)
    (total,) = call(add_kernel, inner, [slope], [], total)
    first, middle = call(middle_kernel, late, [slope, whole], [], full, total)

    early, inner, late = exchange(middle)
    (total,) = call(functools.partial(early_kernel, with_prior=True), early, [slope], [], ham, middle, first)
    (total,) = call(add_kernel, inner, [slope], [], total)
    near, away = call(last_kernel, late, [half_float, half], [pltpu.VMEM((2, levels, levels), float32)], total)
    far = swapped(away, "rep", 1).astype(float32)
    stay = 1.0 - step_size * decay + (0.5 * step_size * step_size) * decay * decay
    is_own = (jnp.arange(2) == rep)[:, None, None]
    outs = []
    for part, state in enumerate((rho_real, rho_imag)):
        change = jnp.where(is_own, near[part][None], far[part][None])
        outs.append(stay[:, None, None] * state + change)
    return tuple(outs)


def solution(mesh):
    axes = Mesh(mesh.devices.reshape(*hier_sizes, mesh.shape["rep"]), (*hier, "rep"))
    placed = (
        P(hier, "rep", None),
        P(hier, "rep", None),
        P(),
        P(),
        P(),
        P(),
        P(),
        P(hier, None),
        P(hier, None),
        P(hier, None),
    )
    return jax.shard_map(
        local,
        mesh=axes,
        in_specs=placed,
        out_specs=(P(hier, "rep", None), P(hier, "rep", None)),
        check_vma=False,
    )
```

```python
import functools

import jax
import jax.numpy as jnp
from jax import lax
from jax.experimental import pallas as pl
from jax.experimental.pallas import tpu as pltpu
from jax.sharding import Mesh, PartitionSpec as P

step_size = 0.1
half_step = 0.5 * step_size
float32 = jnp.float32
bfloat16 = jnp.bfloat16

hier = ("x_lo", "z", "y", "core")
hier_sizes = (2, 16, 4, 2)


def swapped(value, axis, distance):
    pairs = [(source, source ^ distance) for source in range(lax.axis_size(axis))]
    return lax.ppermute(value, axis, pairs)


def across(value, near_core, far_core):
    ring, cores = lax.axis_size("z"), lax.axis_size("core")
    pairs = []
    for source in range(ring):
        for core, target in enumerate((near_core, far_core)):
            if target is not None:
                pairs.append((source * cores + core, target(source) % ring * cores + core))
    return lax.ppermute(value, ("z", "core"), pairs)


def inward(source):
    return source ^ 4


def next_pair(source):
    return source ^ 2


def outward(source):
    return source - 4 if not source & 4 else source + 4


def after(value, *earlier):
    return lax.optimization_barrier((value, *earlier))[0]


def dot(left, right):
    return jnp.dot(left, right, preferred_element_type=float32)


def add_term(total, matrix, real, imag, weight_a, weight_b):
    left_real = dot(matrix, real)
    right_real = dot(real, matrix)
    left_imag = dot(matrix, imag)
    right_imag = dot(imag, matrix)
    total[0] += weight_b * (left_real + right_real) + weight_a * (left_imag - right_imag)
    total[1] += weight_b * (left_imag + right_imag) - weight_a * (left_real - right_real)


def add_commutator(total, ham_ref, real, imag):
    ham_real, ham_imag = ham_ref[0], ham_ref[1]
    total[0] += dot(ham_real, imag) + dot(ham_imag, real) - dot(real, ham_imag) - dot(imag, ham_real)
    total[1] += dot(ham_imag, imag) - dot(ham_real, real) + dot(real, ham_real) - dot(imag, ham_imag)


def rows_of(first, count):
    return pl.ds(pl.multiple_of(first * count, count), count)


def add_bits(total, parts, index_ref, coef_ref, couple_ref, refs, whole):
    for bit, places in parts:
        source = refs[places[0]]
        if len(places) == 2:
            whole[...] = jnp.where(index_ref[10] == 0, source[...], refs[places[1]][...])
            source = whole
        matrix = couple_ref[index_ref[1 + bit]]
        add_term(total, matrix, source[0], source[1], coef_ref[0, bit], coef_ref[1, bit])


def early_kernel(parts, index_ref, coef_ref, couple_ref, ham_ref, own_ref, *refs, with_prior):
    if with_prior:
        prior_ref, *refs = refs
    *partner_refs, total, whole = refs
    if with_prior:
        total[...] = coef_ref[2, 0] * prior_ref[...]
    else:
        total[...] = jnp.zeros_like(total)
    add_commutator(total, ham_ref, own_ref[0], own_ref[1])
    add_bits(total, parts, index_ref, coef_ref, couple_ref, partner_refs, whole)


def add_kernel(parts, index_ref, coef_ref, couple_ref, total_ref, *refs):
    *partner_refs, out_ref, whole = refs
    out_ref[...] = total_ref[...]
    add_bits(out_ref, parts, index_ref, coef_ref, couple_ref, partner_refs, whole)


def middle_kernel(parts, index_ref, coef_ref, couple_ref, own_ref, total_ref, *refs):
    *partner_refs, slope_ref, middle_ref, whole = refs
    slope_ref[...] = total_ref[...]
    add_bits(slope_ref, parts, index_ref, coef_ref, couple_ref, partner_refs, whole)
    middle = coef_ref[2, 0] * own_ref[...].astype(float32) + step_size * slope_ref[...]
    middle_ref[...] = middle.astype(bfloat16)


def last_kernel(parts, index_ref, coef_ref, couple_ref, total_ref, *refs):
    *partner_refs, near_ref, far_ref, whole, total = refs
    total[...] = total_ref[...]
    add_bits(total, parts, index_ref, coef_ref, couple_ref, partner_refs, whole)
    near = index_ref[0]
    rows = near_ref.shape[1]
    near_ref[...] = half_step * total[:, rows_of(near, rows), :]
    far_ref[...] = (half_step * total[:, rows_of(1 - near, rows), :]).astype(bfloat16)


in_vmem = pl.BlockSpec(memory_space=pltpu.VMEM)
in_smem = pl.BlockSpec(memory_space=pltpu.SMEM)


def shaped(kind, *dims):
    return jax.ShapeDtypeStruct(dims, kind)


def local(rho_real, rho_imag, ham, couple, rates, coeff_real, coeff_imag, occupation, upper, lower):
    rep = lax.axis_index("rep")
    rows, levels = rho_real.shape[1:]
    bit_count = lax.axis_size(hier).bit_length()

    own_index = 2 * lax.axis_index(hier) + rep
    occ_float = occupation.astype(float32)
    decay = jnp.sum(occ_float * rates[None, :], axis=1)
    pick = lambda table: jnp.where(rep == 0, table[0], table[1])
    own_occ, own_up, own_low, own_decay = pick(occ_float), pick(upper), pick(lower), pick(decay)
    partner = jnp.bitwise_xor(own_index, jnp.left_shift(1, jnp.arange(bit_count, dtype=jnp.int32)))
    is_above = own_up[None, :] == partner[:, None]
    is_below = own_low[None, :] == partner[:, None]
    mode_range = jnp.arange(couple.shape[0], dtype=jnp.int32)
    modes = jnp.sum(jnp.where(is_above | is_below, mode_range[None, :], 0), axis=1)
    weight_a = jnp.sum(jnp.where(is_above, 1.0, jnp.where(is_below, (own_occ * coeff_real)[None, :], 0.0)), axis=1)
    weight_b = jnp.sum(jnp.where(is_below, (own_occ * coeff_imag)[None, :], 0.0), axis=1)
    keep = 1.0 - step_size * own_decay
    index = jnp.concatenate([rep[None], modes, lax.axis_index("core")[None]]).astype(jnp.int32)
    keeps = jnp.where(jnp.arange(bit_count) < 2, keep, 0.0)
    coef = jnp.stack([weight_a, weight_b, keeps]).astype(float32)

    on_first = lax.axis_index("core") == 0
    whole = shaped(bfloat16, 2, levels, levels)
    slope = shaped(float32, 2, levels, levels)
    half = shaped(bfloat16, 2, rows, levels)
    half_float = shaped(float32, 2, rows, levels)

    def exchange(full):
        p1 = across(full, inward, next_pair)
        core = swapped(full, "core", 1)
        z1 = swapped(full, "z", 1)
        p2 = across(jnp.where(on_first, p1, full), outward, inward)
        x2 = swapped(after(full, p1, core), "rep", 1)
        x1 = swapped(after(full, p1, z1), "x_lo", 1)
        p3 = across(jnp.where(on_first, full, p2), next_pair, outward)
        y2 = swapped(after(full, p2, x2), "y", 2)
        y1 = swapped(after(full, p2, x1), "y", 1)
        return {1: [core], 4: [z1], 8: [x1], 0: [x2]}, {5: [p3, p1], 6: [p1, p2], 7: [p2, p3]}, {3: [y2], 2: [y1]}

    def call(body, parts, outs, scratch, *operands):
        held = []
        places = []
        for bit, arrays in parts.items():
            for array in arrays:
                if not any(array is other for other in held):
                    held.append(array)
            places.append((bit, tuple(next(i for i, x in enumerate(held) if x is array) for array in arrays)))
        arrays = (index, coef, couple, *operands, *held)
        counts = tuple(places)
        moved = sum(x.size * x.dtype.itemsize for x in (*arrays, *outs))
        return pl.pallas_call(
            lambda *refs: body(counts, *refs),
            out_shape=outs,
            in_specs=[in_smem, in_smem] + [in_vmem] * (len(arrays) - 2),
            out_specs=[in_vmem] * len(outs),
            scratch_shapes=[pltpu.VMEM((2, levels, levels), bfloat16), *scratch],
            cost_estimate=pl.CostEstimate(flops=len(parts) * 8 * levels**3, bytes_accessed=moved, transcendentals=0),
            compiler_params=pltpu.CompilerParams(vmem_limit_bytes=12 * 2**20),
        )(*arrays)

    rounded = jnp.stack([rho_real, rho_imag]).astype(bfloat16)
    near = jnp.where(rep == 0, rounded[:, 0], rounded[:, 1])
    away = jnp.where(rep == 0, rounded[:, 1], rounded[:, 0])
    far = swapped(away, "rep", 1)
    full = jnp.where(rep == 0, jnp.concatenate([near, far], axis=1), jnp.concatenate([far, near], axis=1))

    early, inner, late = exchange(full)
    (total,) = call(functools.partial(early_kernel, with_prior=False), early, [slope], [], ham, full)
    (total,) = call(add_kernel, inner, [slope], [], total)
    first, middle = call(middle_kernel, late, [slope, whole], [], full, total)

    early, inner, late = exchange(middle)
    (total,) = call(functools.partial(early_kernel, with_prior=True), early, [slope], [], ham, middle, first)
    (total,) = call(add_kernel, inner, [slope], [], total)
    near, away = call(last_kernel, late, [half_float, half], [pltpu.VMEM((2, levels, levels), float32)], total)
    far = swapped(away, "rep", 1).astype(float32)
    stay = 1.0 - step_size * decay + (0.5 * step_size * step_size) * decay * decay
    is_own = (jnp.arange(2) == rep)[:, None, None]
    outs = []
    for part, state in enumerate((rho_real, rho_imag)):
        change = jnp.where(is_own, near[part][None], far[part][None])
        outs.append(stay[:, None, None] * state + change)
    return tuple(outs)


def solution(mesh):
    axes = Mesh(mesh.devices.reshape(*hier_sizes, mesh.shape["rep"]), (*hier, "rep"))
    placed = (
        P(hier, "rep", None),
        P(hier, "rep", None),
        P(),
        P(),
        P(),
        P(),
        P(),
        P(hier, None),
        P(hier, None),
        P(hier, None),
    )
    return jax.shard_map(
        local,
        mesh=axes,
        in_specs=placed,
        out_specs=(P(hier, "rep", None), P(hier, "rep", None)),
        check_vma=False,
    )
```

```python
import functools

import jax
import jax.numpy as jnp
from jax import lax
from jax.experimental import pallas as pl
from jax.experimental.pallas import tpu as pltpu
from jax.sharding import Mesh, PartitionSpec as P

step_size = 0.1
half_step = 0.5 * step_size
float32 = jnp.float32
bfloat16 = jnp.bfloat16

hier = ("x_lo", "z", "y", "core")
hier_sizes = (2, 16, 4, 2)


def swapped(value, axis, distance):
    pairs = [(source, source ^ distance) for source in range(lax.axis_size(axis))]
    return lax.ppermute(value, axis, pairs)


def across(value, near_core, far_core):
    ring, cores = lax.axis_size("z"), lax.axis_size("core")
    pairs = []
    for source in range(ring):
        for core, target in enumerate((near_core, far_core)):
            if target is not None:
                pairs.append((source * cores + core, target(source) % ring * cores + core))
    return lax.ppermute(value, ("z", "core"), pairs)


def inward(source):
    return source ^ 4


def outward(source):
    return source - 4 if not source & 4 else source + 4


def after(value, *earlier):
    return lax.optimization_barrier((value, *earlier))[0]


def dot(left, right):
    return jnp.dot(left, right, preferred_element_type=float32)


def add_term(total, matrix, real, imag, weight_a, weight_b):
    left_real = dot(matrix, real)
    right_real = dot(real, matrix)
    left_imag = dot(matrix, imag)
    right_imag = dot(imag, matrix)
    total[0] += weight_b * (left_real + right_real) + weight_a * (left_imag - right_imag)
    total[1] += weight_b * (left_imag + right_imag) - weight_a * (left_real - right_real)


def add_commutator(total, ham_ref, real, imag):
    ham_real, ham_imag = ham_ref[0], ham_ref[1]
    total[0] += dot(ham_real, imag) + dot(ham_imag, real) - dot(real, ham_imag) - dot(imag, ham_real)
    total[1] += dot(ham_imag, imag) - dot(ham_real, real) + dot(real, ham_real) - dot(imag, ham_imag)


def rows_of(first, count):
    return pl.ds(pl.multiple_of(first * count, count), count)


def add_bits(total, parts, index_ref, coef_ref, couple_ref, refs, whole):
    for bit, places in parts:
        source = refs[places[0]]
        if len(places) == 2:
            whole[...] = jnp.where(index_ref[10] == 0, source[...], refs[places[1]][...])
            source = whole
        matrix = couple_ref[index_ref[1 + bit]]
        add_term(total, matrix, source[0], source[1], coef_ref[0, bit], coef_ref[1, bit])


def early_kernel(parts, index_ref, coef_ref, couple_ref, ham_ref, own_ref, *refs, with_prior):
    if with_prior:
        prior_ref, *refs = refs
    *partner_refs, total, whole = refs
    if with_prior:
        total[...] = coef_ref[2, 0] * prior_ref[...]
    else:
        total[...] = jnp.zeros_like(total)
    add_commutator(total, ham_ref, own_ref[0], own_ref[1])
    add_bits(total, parts, index_ref, coef_ref, couple_ref, partner_refs, whole)


def add_kernel(parts, index_ref, coef_ref, couple_ref, total_ref, *refs):
    *partner_refs, out_ref, whole = refs
    out_ref[...] = total_ref[...]
    add_bits(out_ref, parts, index_ref, coef_ref, couple_ref, partner_refs, whole)


def middle_kernel(parts, index_ref, coef_ref, couple_ref, own_ref, total_ref, *refs):
    *partner_refs, slope_ref, middle_ref, whole = refs
    slope_ref[...] = total_ref[...]
    add_bits(slope_ref, parts, index_ref, coef_ref, couple_ref, partner_refs, whole)
    middle = coef_ref[2, 0] * own_ref[...].astype(float32) + step_size * slope_ref[...]
    middle_ref[...] = middle.astype(bfloat16)


def last_kernel(parts, index_ref, coef_ref, couple_ref, total_ref, *refs):
    *partner_refs, near_ref, far_ref, whole, total = refs
    total[...] = total_ref[...]
    add_bits(total, parts, index_ref, coef_ref, couple_ref, partner_refs, whole)
    near = index_ref[0]
    rows = near_ref.shape[1]
    near_ref[...] = half_step * total[:, rows_of(near, rows), :]
    far_ref[...] = (half_step * total[:, rows_of(1 - near, rows), :]).astype(bfloat16)


in_vmem = pl.BlockSpec(memory_space=pltpu.VMEM)
in_smem = pl.BlockSpec(memory_space=pltpu.SMEM)


def shaped(kind, *dims):
    return jax.ShapeDtypeStruct(dims, kind)


def local(rho_real, rho_imag, ham, couple, rates, coeff_real, coeff_imag, occupation, upper, lower):
    rep = lax.axis_index("rep")
    rows, levels = rho_real.shape[1:]
    bit_count = lax.axis_size(hier).bit_length()

    own_index = 2 * lax.axis_index(hier) + rep
    occ_float = occupation.astype(float32)
    decay = jnp.sum(occ_float * rates[None, :], axis=1)
    pick = lambda table: jnp.where(rep == 0, table[0], table[1])
    own_occ, own_up, own_low, own_decay = pick(occ_float), pick(upper), pick(lower), pick(decay)
    partner = jnp.bitwise_xor(own_index, jnp.left_shift(1, jnp.arange(bit_count, dtype=jnp.int32)))
    is_above = own_up[None, :] == partner[:, None]
    is_below = own_low[None, :] == partner[:, None]
    mode_range = jnp.arange(couple.shape[0], dtype=jnp.int32)
    modes = jnp.sum(jnp.where(is_above | is_below, mode_range[None, :], 0), axis=1)
    weight_a = jnp.sum(jnp.where(is_above, 1.0, jnp.where(is_below, (own_occ * coeff_real)[None, :], 0.0)), axis=1)
    weight_b = jnp.sum(jnp.where(is_below, (own_occ * coeff_imag)[None, :], 0.0), axis=1)
    keep = 1.0 - step_size * own_decay
    index = jnp.concatenate([rep[None], modes, lax.axis_index("core")[None]]).astype(jnp.int32)
    keeps = jnp.where(jnp.arange(bit_count) < 2, keep, 0.0)
    coef = jnp.stack([weight_a, weight_b, keeps]).astype(float32)

    whole = shaped(bfloat16, 2, levels, levels)
    slope = shaped(float32, 2, levels, levels)
    half = shaped(bfloat16, 2, rows, levels)
    half_float = shaped(float32, 2, rows, levels)

    def exchange(full):
        first = across(full, inward, outward)
        own = across(full, None, inward)
        core = swapped(full, "core", 1)
        z2 = swapped(full, "z", 2)
        second = across(first, outward, inward)
        z1 = swapped(after(full, first, core), "z", 1)
        x2 = swapped(after(full, first, core), "rep", 1)
        x1 = swapped(after(full, first, own), "x_lo", 1)
        y2 = swapped(after(full, first, own), "y", 2)
        y1 = swapped(after(full, first, z2, z1), "y", 1)
        return {1: [core], 5: [z2]}, {6: [first, own], 7: [second], 4: [z1]}, {0: [x2], 8: [x1], 3: [y2], 2: [y1]}

    def call(body, parts, outs, scratch, *operands):
        held = []
        places = []
        for bit, arrays in parts.items():
            for array in arrays:
                if not any(array is other for other in held):
                    held.append(array)
            places.append((bit, tuple(next(i for i, x in enumerate(held) if x is array) for array in arrays)))
        arrays = (index, coef, couple, *operands, *held)
        counts = tuple(places)
        moved = sum(x.size * x.dtype.itemsize for x in (*arrays, *outs))
        return pl.pallas_call(
            lambda *refs: body(counts, *refs),
            out_shape=outs,
            in_specs=[in_smem, in_smem] + [in_vmem] * (len(arrays) - 2),
            out_specs=[in_vmem] * len(outs),
            scratch_shapes=[pltpu.VMEM((2, levels, levels), bfloat16), *scratch],
            cost_estimate=pl.CostEstimate(flops=len(parts) * 8 * levels**3, bytes_accessed=moved, transcendentals=0),
            compiler_params=pltpu.CompilerParams(vmem_limit_bytes=12 * 2**20),
        )(*arrays)

    rounded = jnp.stack([rho_real, rho_imag]).astype(bfloat16)
    near = jnp.where(rep == 0, rounded[:, 0], rounded[:, 1])
    away = jnp.where(rep == 0, rounded[:, 1], rounded[:, 0])
    far = swapped(away, "rep", 1)
    full = jnp.where(rep == 0, jnp.concatenate([near, far], axis=1), jnp.concatenate([far, near], axis=1))

    early, inner, late = exchange(full)
    (total,) = call(functools.partial(early_kernel, with_prior=False), early, [slope], [], ham, full)
    (total,) = call(add_kernel, inner, [slope], [], total)
    first, middle = call(middle_kernel, late, [slope, whole], [], full, total)

    early, inner, late = exchange(middle)
    (total,) = call(functools.partial(early_kernel, with_prior=True), early, [slope], [], ham, middle, first)
    (total,) = call(add_kernel, inner, [slope], [], total)
    near, away = call(last_kernel, late, [half_float, half], [pltpu.VMEM((2, levels, levels), float32)], total)
    far = swapped(away, "rep", 1).astype(float32)
    stay = 1.0 - step_size * decay + (0.5 * step_size * step_size) * decay * decay
    is_own = (jnp.arange(2) == rep)[:, None, None]
    outs = []
    for part, state in enumerate((rho_real, rho_imag)):
        change = jnp.where(is_own, near[part][None], far[part][None])
        outs.append(stay[:, None, None] * state + change)
    return tuple(outs)


def solution(mesh):
    axes = Mesh(mesh.devices.reshape(*hier_sizes, mesh.shape["rep"]), (*hier, "rep"))
    placed = (
        P(hier, "rep", None),
        P(hier, "rep", None),
        P(),
        P(),
        P(),
        P(),
        P(),
        P(hier, None),
        P(hier, None),
        P(hier, None),
    )
    return jax.shard_map(
        local,
        mesh=axes,
        in_specs=placed,
        out_specs=(P(hier, "rep", None), P(hier, "rep", None)),
        check_vma=False,
    )
```

```python
import functools

import jax
import jax.numpy as jnp
from jax import lax
from jax.experimental import pallas as pl
from jax.experimental.pallas import tpu as pltpu
from jax.sharding import Mesh, PartitionSpec as P

step_size = 0.1
half_step = 0.5 * step_size
float32 = jnp.float32
bfloat16 = jnp.bfloat16

hier = ("x_lo", "z", "y", "core")
hier_sizes = (2, 16, 4, 2)


def swapped(value, axis, distance):
    pairs = [(source, source ^ distance) for source in range(lax.axis_size(axis))]
    return lax.ppermute(value, axis, pairs)


def across(value, near_core, far_core):
    ring, cores = lax.axis_size("z"), lax.axis_size("core")
    pairs = []
    for source in range(ring):
        for core, target in enumerate((near_core, far_core)):
            if target is not None:
                pairs.append((source * cores + core, target(source) % ring * cores + core))
    return lax.ppermute(value, ("z", "core"), pairs)


def inward(source):
    return source ^ 4


def opposite(source):
    return source ^ 8


def outward(source):
    return source - 4 if not source & 4 else source + 4


def after(value, *earlier):
    return lax.optimization_barrier((value, *earlier))[0]


def dot(left, right):
    return jnp.dot(left, right, preferred_element_type=float32)


def add_term(total, matrix, real, imag, weight_a, weight_b):
    left_real = dot(matrix, real)
    right_real = dot(real, matrix)
    left_imag = dot(matrix, imag)
    right_imag = dot(imag, matrix)
    total[0] += weight_b * (left_real + right_real) + weight_a * (left_imag - right_imag)
    total[1] += weight_b * (left_imag + right_imag) - weight_a * (left_real - right_real)


def add_commutator(total, ham_ref, real, imag):
    ham_real, ham_imag = ham_ref[0], ham_ref[1]
    total[0] += dot(ham_real, imag) + dot(ham_imag, real) - dot(real, ham_imag) - dot(imag, ham_real)
    total[1] += dot(ham_imag, imag) - dot(ham_real, real) + dot(real, ham_real) - dot(imag, ham_imag)


def rows_of(first, count):
    return pl.ds(pl.multiple_of(first * count, count), count)


def add_bits(total, parts, index_ref, coef_ref, couple_ref, refs, whole):
    for bit, places in parts:
        source = refs[places[0]]
        if len(places) == 2:
            whole[...] = jnp.where(index_ref[10] == 0, source[...], refs[places[1]][...])
            source = whole
        matrix = couple_ref[index_ref[1 + bit]]
        add_term(total, matrix, source[0], source[1], coef_ref[0, bit], coef_ref[1, bit])


def early_kernel(parts, index_ref, coef_ref, couple_ref, ham_ref, own_ref, *refs, with_prior):
    if with_prior:
        prior_ref, *refs = refs
    *partner_refs, total, whole = refs
    if with_prior:
        total[...] = coef_ref[2, 0] * prior_ref[...]
    else:
        total[...] = jnp.zeros_like(total)
    add_commutator(total, ham_ref, own_ref[0], own_ref[1])
    add_bits(total, parts, index_ref, coef_ref, couple_ref, partner_refs, whole)


def add_kernel(parts, index_ref, coef_ref, couple_ref, total_ref, *refs):
    *partner_refs, out_ref, whole = refs
    out_ref[...] = total_ref[...]
    add_bits(out_ref, parts, index_ref, coef_ref, couple_ref, partner_refs, whole)


def middle_kernel(parts, index_ref, coef_ref, couple_ref, own_ref, total_ref, *refs):
    *partner_refs, slope_ref, middle_ref, whole = refs
    slope_ref[...] = total_ref[...]
    add_bits(slope_ref, parts, index_ref, coef_ref, couple_ref, partner_refs, whole)
    middle = coef_ref[2, 0] * own_ref[...].astype(float32) + step_size * slope_ref[...]
    middle_ref[...] = middle.astype(bfloat16)


def last_kernel(parts, index_ref, coef_ref, couple_ref, total_ref, *refs):
    *partner_refs, near_ref, far_ref, whole, total = refs
    total[...] = total_ref[...]
    add_bits(total, parts, index_ref, coef_ref, couple_ref, partner_refs, whole)
    near = index_ref[0]
    rows = near_ref.shape[1]
    near_ref[...] = half_step * total[:, rows_of(near, rows), :]
    far_ref[...] = (half_step * total[:, rows_of(1 - near, rows), :]).astype(bfloat16)


in_vmem = pl.BlockSpec(memory_space=pltpu.VMEM)
in_smem = pl.BlockSpec(memory_space=pltpu.SMEM)


def shaped(kind, *dims):
    return jax.ShapeDtypeStruct(dims, kind)


def local(rho_real, rho_imag, ham, couple, rates, coeff_real, coeff_imag, occupation, upper, lower):
    rep = lax.axis_index("rep")
    rows, levels = rho_real.shape[1:]
    bit_count = lax.axis_size(hier).bit_length()

    own_index = 2 * lax.axis_index(hier) + rep
    occ_float = occupation.astype(float32)
    decay = jnp.sum(occ_float * rates[None, :], axis=1)
    pick = lambda table: jnp.where(rep == 0, table[0], table[1])
    own_occ, own_up, own_low, own_decay = pick(occ_float), pick(upper), pick(lower), pick(decay)
    partner = jnp.bitwise_xor(own_index, jnp.left_shift(1, jnp.arange(bit_count, dtype=jnp.int32)))
    is_above = own_up[None, :] == partner[:, None]
    is_below = own_low[None, :] == partner[:, None]
    mode_range = jnp.arange(couple.shape[0], dtype=jnp.int32)
    modes = jnp.sum(jnp.where(is_above | is_below, mode_range[None, :], 0), axis=1)
    weight_a = jnp.sum(jnp.where(is_above, 1.0, jnp.where(is_below, (own_occ * coeff_real)[None, :], 0.0)), axis=1)
    weight_b = jnp.sum(jnp.where(is_below, (own_occ * coeff_imag)[None, :], 0.0), axis=1)
    keep = 1.0 - step_size * own_decay
    index = jnp.concatenate([rep[None], modes, lax.axis_index("core")[None]]).astype(jnp.int32)
    keeps = jnp.where(jnp.arange(bit_count) < 2, keep, 0.0)
    coef = jnp.stack([weight_a, weight_b, keeps]).astype(float32)

    on_first = lax.axis_index("core") == 0
    whole = shaped(bfloat16, 2, levels, levels)
    slope = shaped(float32, 2, levels, levels)
    half = shaped(bfloat16, 2, rows, levels)
    half_float = shaped(float32, 2, rows, levels)

    def exchange(full):
        first = across(full, inward, opposite)
        core = swapped(full, "core", 1)
        x2 = swapped(full, "rep", 1)
        y2 = swapped(full, "y", 2)
        x1 = swapped(full, "x_lo", 1)
        second = across(jnp.where(on_first, first, full), outward, inward)
        z2 = swapped(after(full, first, core), "z", 2)
        z1 = swapped(after(full, first, x2), "z", 1)
        y1 = swapped(after(full, first, y2), "y", 1)
        return {1: [core], 0: [x2], 3: [y2], 8: [x1]}, {6: [first, second], 7: [second, first]}, {5: [z2], 4: [z1], 2: [y1]}

    def call(body, parts, outs, scratch, *operands):
        held = []
        places = []
        for bit, arrays in parts.items():
            for array in arrays:
                if not any(array is other for other in held):
                    held.append(array)
            places.append((bit, tuple(next(i for i, x in enumerate(held) if x is array) for array in arrays)))
        arrays = (index, coef, couple, *operands, *held)
        counts = tuple(places)
        moved = sum(x.size * x.dtype.itemsize for x in (*arrays, *outs))
        return pl.pallas_call(
            lambda *refs: body(counts, *refs),
            out_shape=outs,
            in_specs=[in_smem, in_smem] + [in_vmem] * (len(arrays) - 2),
            out_specs=[in_vmem] * len(outs),
            scratch_shapes=[pltpu.VMEM((2, levels, levels), bfloat16), *scratch],
            cost_estimate=pl.CostEstimate(flops=len(parts) * 8 * levels**3, bytes_accessed=moved, transcendentals=0),
            compiler_params=pltpu.CompilerParams(vmem_limit_bytes=12 * 2**20),
        )(*arrays)

    rounded = jnp.stack([rho_real, rho_imag]).astype(bfloat16)
    near = jnp.where(rep == 0, rounded[:, 0], rounded[:, 1])
    away = jnp.where(rep == 0, rounded[:, 1], rounded[:, 0])
    far = swapped(away, "rep", 1)
    full = jnp.where(rep == 0, jnp.concatenate([near, far], axis=1), jnp.concatenate([far, near], axis=1))

    early, inner, late = exchange(full)
    (total,) = call(functools.partial(early_kernel, with_prior=False), early, [slope], [], ham, full)
    (total,) = call(add_kernel, inner, [slope], [], total)
    first, middle = call(middle_kernel, late, [slope, whole], [], full, total)

    early, inner, late = exchange(middle)
    (total,) = call(functools.partial(early_kernel, with_prior=True), early, [slope], [], ham, middle, first)
    (total,) = call(add_kernel, inner, [slope], [], total)
    near, away = call(last_kernel, late, [half_float, half], [pltpu.VMEM((2, levels, levels), float32)], total)
    far = swapped(away, "rep", 1).astype(float32)
    stay = 1.0 - step_size * decay + (0.5 * step_size * step_size) * decay * decay
    is_own = (jnp.arange(2) == rep)[:, None, None]
    outs = []
    for part, state in enumerate((rho_real, rho_imag)):
        change = jnp.where(is_own, near[part][None], far[part][None])
        outs.append(stay[:, None, None] * state + change)
    return tuple(outs)


def solution(mesh):
    axes = Mesh(mesh.devices.reshape(*hier_sizes, mesh.shape["rep"]), (*hier, "rep"))
    placed = (
        P(hier, "rep", None),
        P(hier, "rep", None),
        P(),
        P(),
        P(),
        P(),
        P(),
        P(hier, None),
        P(hier, None),
        P(hier, None),
    )
    return jax.shard_map(
        local,
        mesh=axes,
        in_specs=placed,
        out_specs=(P(hier, "rep", None), P(hier, "rep", None)),
        check_vma=False,
    )
```

```python
import functools

import jax
import jax.numpy as jnp
from jax import lax
from jax.experimental import pallas as pl
from jax.experimental.pallas import tpu as pltpu
from jax.sharding import Mesh, PartitionSpec as P

step_size = 0.1
half_step = 0.5 * step_size
float32 = jnp.float32
bfloat16 = jnp.bfloat16

hier = ("x_lo", "z", "y", "core")
hier_sizes = (2, 16, 4, 2)


def swapped(value, axis, distance):
    pairs = [(source, source ^ distance) for source in range(lax.axis_size(axis))]
    return lax.ppermute(value, axis, pairs)


def across(value, near_core, far_core):
    ring, cores = lax.axis_size("z"), lax.axis_size("core")
    pairs = []
    for source in range(ring):
        for core, target in enumerate((near_core, far_core)):
            if target is not None:
                pairs.append((source * cores + core, target(source) % ring * cores + core))
    return lax.ppermute(value, ("z", "core"), pairs)


def inward(source):
    return source ^ 4


def outward(source):
    return source - 4 if not source & 4 else source + 4


def after(value, *earlier):
    return lax.optimization_barrier((value, *earlier))[0]


def dot(left, right):
    return jnp.dot(left, right, preferred_element_type=float32)


def add_term(total, matrix, real, imag, weight_a, weight_b):
    left_real = dot(matrix, real)
    right_real = dot(real, matrix)
    left_imag = dot(matrix, imag)
    right_imag = dot(imag, matrix)
    total[0] += weight_b * (left_real + right_real) + weight_a * (left_imag - right_imag)
    total[1] += weight_b * (left_imag + right_imag) - weight_a * (left_real - right_real)


def add_commutator(total, ham_ref, real, imag):
    ham_real, ham_imag = ham_ref[0], ham_ref[1]
    total[0] += dot(ham_real, imag) + dot(ham_imag, real) - dot(real, ham_imag) - dot(imag, ham_real)
    total[1] += dot(ham_imag, imag) - dot(ham_real, real) + dot(real, ham_real) - dot(imag, ham_imag)


def rows_of(first, count):
    return pl.ds(pl.multiple_of(first * count, count), count)


def add_bits(total, parts, index_ref, coef_ref, couple_ref, refs, whole):
    for bit, places in parts:
        source = refs[places[0]]
        if len(places) == 2:
            whole[...] = jnp.where(index_ref[10] == 0, source[...], refs[places[1]][...])
            source = whole
        matrix = couple_ref[index_ref[1 + bit]]
        add_term(total, matrix, source[0], source[1], coef_ref[0, bit], coef_ref[1, bit])


def early_kernel(parts, index_ref, coef_ref, couple_ref, ham_ref, own_ref, *refs, with_prior):
    if with_prior:
        prior_ref, *refs = refs
    *partner_refs, total, whole = refs
    if with_prior:
        total[...] = coef_ref[2, 0] * prior_ref[...]
    else:
        total[...] = jnp.zeros_like(total)
    add_commutator(total, ham_ref, own_ref[0], own_ref[1])
    add_bits(total, parts, index_ref, coef_ref, couple_ref, partner_refs, whole)


def add_kernel(parts, index_ref, coef_ref, couple_ref, total_ref, *refs):
    *partner_refs, out_ref, whole = refs
    out_ref[...] = total_ref[...]
    add_bits(out_ref, parts, index_ref, coef_ref, couple_ref, partner_refs, whole)


def middle_kernel(parts, index_ref, coef_ref, couple_ref, own_ref, total_ref, *refs):
    *partner_refs, slope_ref, middle_ref, whole = refs
    slope_ref[...] = total_ref[...]
    add_bits(slope_ref, parts, index_ref, coef_ref, couple_ref, partner_refs, whole)
    middle = coef_ref[2, 0] * own_ref[...].astype(float32) + step_size * slope_ref[...]
    middle_ref[...] = middle.astype(bfloat16)


def last_kernel(parts, index_ref, coef_ref, couple_ref, total_ref, *refs):
    *partner_refs, near_ref, far_ref, whole, total = refs
    total[...] = total_ref[...]
    add_bits(total, parts, index_ref, coef_ref, couple_ref, partner_refs, whole)
    near = index_ref[0]
    rows = near_ref.shape[1]
    near_ref[...] = half_step * total[:, rows_of(near, rows), :]
    far_ref[...] = (half_step * total[:, rows_of(1 - near, rows), :]).astype(bfloat16)


in_vmem = pl.BlockSpec(memory_space=pltpu.VMEM)
in_smem = pl.BlockSpec(memory_space=pltpu.SMEM)


def shaped(kind, *dims):
    return jax.ShapeDtypeStruct(dims, kind)


def local(rho_real, rho_imag, ham, couple, rates, coeff_real, coeff_imag, occupation, upper, lower):
    rep = lax.axis_index("rep")
    rows, levels = rho_real.shape[1:]
    bit_count = lax.axis_size(hier).bit_length()

    own_index = 2 * lax.axis_index(hier) + rep
    occ_float = occupation.astype(float32)
    decay = jnp.sum(occ_float * rates[None, :], axis=1)
    pick = lambda table: jnp.where(rep == 0, table[0], table[1])
    own_occ, own_up, own_low, own_decay = pick(occ_float), pick(upper), pick(lower), pick(decay)
    partner = jnp.bitwise_xor(own_index, jnp.left_shift(1, jnp.arange(bit_count, dtype=jnp.int32)))
    is_above = own_up[None, :] == partner[:, None]
    is_below = own_low[None, :] == partner[:, None]
    mode_range = jnp.arange(couple.shape[0], dtype=jnp.int32)
    modes = jnp.sum(jnp.where(is_above | is_below, mode_range[None, :], 0), axis=1)
    weight_a = jnp.sum(jnp.where(is_above, 1.0, jnp.where(is_below, (own_occ * coeff_real)[None, :], 0.0)), axis=1)
    weight_b = jnp.sum(jnp.where(is_below, (own_occ * coeff_imag)[None, :], 0.0), axis=1)
    keep = 1.0 - step_size * own_decay
    index = jnp.concatenate([rep[None], modes, lax.axis_index("core")[None]]).astype(jnp.int32)
    keeps = jnp.where(jnp.arange(bit_count) < 2, keep, 0.0)
    coef = jnp.stack([weight_a, weight_b, keeps]).astype(float32)

    whole = shaped(bfloat16, 2, levels, levels)
    slope = shaped(float32, 2, levels, levels)
    half = shaped(bfloat16, 2, rows, levels)
    half_float = shaped(float32, 2, rows, levels)

    def exchange(full):
        first = across(full, inward, outward)
        z1 = swapped(full, "z", 1)
        core = swapped(full, "core", 1)
        z2 = swapped(full, "z", 2)
        own = across(full, None, inward)
        x2 = swapped(after(full, z1), "rep", 1)
        x1 = swapped(after(full, core), "x_lo", 1)
        second = across(first, outward, inward)
        y2 = swapped(after(full, first, x2), "y", 2)
        y1 = swapped(after(full, first, x1), "y", 1)
        return {1: [core], 4: [z1], 5: [z2], 8: [x1], 0: [x2], 6: [first, own]}, {7: [second]}, {3: [y2], 2: [y1]}

    def call(body, parts, outs, scratch, *operands):
        held = []
        places = []
        for bit, arrays in parts.items():
            for array in arrays:
                if not any(array is other for other in held):
                    held.append(array)
            places.append((bit, tuple(next(i for i, x in enumerate(held) if x is array) for array in arrays)))
        arrays = (index, coef, couple, *operands, *held)
        counts = tuple(places)
        moved = sum(x.size * x.dtype.itemsize for x in (*arrays, *outs))
        return pl.pallas_call(
            lambda *refs: body(counts, *refs),
            out_shape=outs,
            in_specs=[in_smem, in_smem] + [in_vmem] * (len(arrays) - 2),
            out_specs=[in_vmem] * len(outs),
            scratch_shapes=[pltpu.VMEM((2, levels, levels), bfloat16), *scratch],
            cost_estimate=pl.CostEstimate(flops=len(parts) * 8 * levels**3, bytes_accessed=moved, transcendentals=0),
            compiler_params=pltpu.CompilerParams(vmem_limit_bytes=12 * 2**20),
        )(*arrays)

    rounded = jnp.stack([rho_real, rho_imag]).astype(bfloat16)
    near = jnp.where(rep == 0, rounded[:, 0], rounded[:, 1])
    away = jnp.where(rep == 0, rounded[:, 1], rounded[:, 0])
    far = swapped(away, "rep", 1)
    full = jnp.where(rep == 0, jnp.concatenate([near, far], axis=1), jnp.concatenate([far, near], axis=1))

    early, inner, late = exchange(full)
    (total,) = call(functools.partial(early_kernel, with_prior=False), early, [slope], [], ham, full)
    (total,) = call(add_kernel, inner, [slope], [], total)
    first, middle = call(middle_kernel, late, [slope, whole], [], full, total)

    early, inner, late = exchange(middle)
    (total,) = call(functools.partial(early_kernel, with_prior=True), early, [slope], [], ham, middle, first)
    (total,) = call(add_kernel, inner, [slope], [], total)
    near, away = call(last_kernel, late, [half_float, half], [pltpu.VMEM((2, levels, levels), float32)], total)
    far = swapped(away, "rep", 1).astype(float32)
    stay = 1.0 - step_size * decay + (0.5 * step_size * step_size) * decay * decay
    is_own = (jnp.arange(2) == rep)[:, None, None]
    outs = []
    for part, state in enumerate((rho_real, rho_imag)):
        change = jnp.where(is_own, near[part][None], far[part][None])
        outs.append(stay[:, None, None] * state + change)
    return tuple(outs)


def solution(mesh):
    axes = Mesh(mesh.devices.reshape(*hier_sizes, mesh.shape["rep"]), (*hier, "rep"))
    placed = (
        P(hier, "rep", None),
        P(hier, "rep", None),
        P(),
        P(),
        P(),
        P(),
        P(),
        P(hier, None),
        P(hier, None),
        P(hier, None),
    )
    return jax.shard_map(
        local,
        mesh=axes,
        in_specs=placed,
        out_specs=(P(hier, "rep", None), P(hier, "rep", None)),
        check_vma=False,
    )
```

```python
import functools

import jax
import jax.numpy as jnp
from jax import lax
from jax.experimental import pallas as pl
from jax.experimental.pallas import tpu as pltpu
from jax.sharding import Mesh, PartitionSpec as P

step_size = 0.1
half_step = 0.5 * step_size
float32 = jnp.float32
bfloat16 = jnp.bfloat16

hier = ("x_lo", "z", "y", "core")
hier_sizes = (2, 16, 4, 2)


def swapped(value, axis, distance):
    pairs = [(source, source ^ distance) for source in range(lax.axis_size(axis))]
    return lax.ppermute(value, axis, pairs)


def across(value, near_core, far_core):
    ring, cores = lax.axis_size("z"), lax.axis_size("core")
    pairs = []
    for source in range(ring):
        for core, target in enumerate((near_core, far_core)):
            if target is not None:
                pairs.append((source * cores + core, target(source) % ring * cores + core))
    return lax.ppermute(value, ("z", "core"), pairs)


def inward(source):
    return source ^ 4


def opposite(source):
    return source ^ 8


def outward(source):
    return source - 4 if not source & 4 else source + 4


def after(value, *earlier):
    return lax.optimization_barrier((value, *earlier))[0]


def dot(left, right):
    return jnp.dot(left, right, preferred_element_type=float32)


def add_term(total, matrix, real, imag, weight_a, weight_b):
    left_real = dot(matrix, real)
    right_real = dot(real, matrix)
    left_imag = dot(matrix, imag)
    right_imag = dot(imag, matrix)
    total[0] += weight_b * (left_real + right_real) + weight_a * (left_imag - right_imag)
    total[1] += weight_b * (left_imag + right_imag) - weight_a * (left_real - right_real)


def add_commutator(total, ham_ref, real, imag):
    ham_real, ham_imag = ham_ref[0], ham_ref[1]
    total[0] += dot(ham_real, imag) + dot(ham_imag, real) - dot(real, ham_imag) - dot(imag, ham_real)
    total[1] += dot(ham_imag, imag) - dot(ham_real, real) + dot(real, ham_real) - dot(imag, ham_imag)


def rows_of(first, count):
    return pl.ds(pl.multiple_of(first * count, count), count)


def add_bits(total, parts, index_ref, coef_ref, couple_ref, refs, whole):
    for bit, places in parts:
        source = refs[places[0]]
        if len(places) == 2:
            whole[...] = jnp.where(index_ref[10] == 0, source[...], refs[places[1]][...])
            source = whole
        matrix = couple_ref[index_ref[1 + bit]]
        add_term(total, matrix, source[0], source[1], coef_ref[0, bit], coef_ref[1, bit])


def early_kernel(parts, index_ref, coef_ref, couple_ref, ham_ref, own_ref, *refs, with_prior):
    if with_prior:
        prior_ref, *refs = refs
    *partner_refs, total, whole = refs
    if with_prior:
        total[...] = coef_ref[2, 0] * prior_ref[...]
    else:
        total[...] = jnp.zeros_like(total)
    add_commutator(total, ham_ref, own_ref[0], own_ref[1])
    add_bits(total, parts, index_ref, coef_ref, couple_ref, partner_refs, whole)


def add_kernel(parts, index_ref, coef_ref, couple_ref, total_ref, *refs):
    *partner_refs, out_ref, whole = refs
    out_ref[...] = total_ref[...]
    add_bits(out_ref, parts, index_ref, coef_ref, couple_ref, partner_refs, whole)


def middle_kernel(parts, index_ref, coef_ref, couple_ref, own_ref, total_ref, *refs):
    *partner_refs, slope_ref, middle_ref, whole = refs
    slope_ref[...] = total_ref[...]
    add_bits(slope_ref, parts, index_ref, coef_ref, couple_ref, partner_refs, whole)
    middle = coef_ref[2, 0] * own_ref[...].astype(float32) + step_size * slope_ref[...]
    middle_ref[...] = middle.astype(bfloat16)


def last_kernel(parts, index_ref, coef_ref, couple_ref, total_ref, *refs):
    *partner_refs, near_ref, far_ref, whole, total = refs
    total[...] = total_ref[...]
    add_bits(total, parts, index_ref, coef_ref, couple_ref, partner_refs, whole)
    near = index_ref[0]
    rows = near_ref.shape[1]
    near_ref[...] = half_step * total[:, rows_of(near, rows), :]
    far_ref[...] = (half_step * total[:, rows_of(1 - near, rows), :]).astype(bfloat16)


in_vmem = pl.BlockSpec(memory_space=pltpu.VMEM)
in_smem = pl.BlockSpec(memory_space=pltpu.SMEM)


def shaped(kind, *dims):
    return jax.ShapeDtypeStruct(dims, kind)


def local(rho_real, rho_imag, ham, couple, rates, coeff_real, coeff_imag, occupation, upper, lower):
    rep = lax.axis_index("rep")
    rows, levels = rho_real.shape[1:]
    bit_count = lax.axis_size(hier).bit_length()

    own_index = 2 * lax.axis_index(hier) + rep
    occ_float = occupation.astype(float32)
    decay = jnp.sum(occ_float * rates[None, :], axis=1)
    pick = lambda table: jnp.where(rep == 0, table[0], table[1])
    own_occ, own_up, own_low, own_decay = pick(occ_float), pick(upper), pick(lower), pick(decay)
    partner = jnp.bitwise_xor(own_index, jnp.left_shift(1, jnp.arange(bit_count, dtype=jnp.int32)))
    is_above = own_up[None, :] == partner[:, None]
    is_below = own_low[None, :] == partner[:, None]
    mode_range = jnp.arange(couple.shape[0], dtype=jnp.int32)
    modes = jnp.sum(jnp.where(is_above | is_below, mode_range[None, :], 0), axis=1)
    weight_a = jnp.sum(jnp.where(is_above, 1.0, jnp.where(is_below, (own_occ * coeff_real)[None, :], 0.0)), axis=1)
    weight_b = jnp.sum(jnp.where(is_below, (own_occ * coeff_imag)[None, :], 0.0), axis=1)
    keep = 1.0 - step_size * own_decay
    index = jnp.concatenate([rep[None], modes, lax.axis_index("core")[None]]).astype(jnp.int32)
    keeps = jnp.where(jnp.arange(bit_count) < 2, keep, 0.0)
    coef = jnp.stack([weight_a, weight_b, keeps]).astype(float32)

    on_first = lax.axis_index("core") == 0
    whole = shaped(bfloat16, 2, levels, levels)
    slope = shaped(float32, 2, levels, levels)
    half = shaped(bfloat16, 2, rows, levels)
    half_float = shaped(float32, 2, rows, levels)

    def exchange(full):
        first = across(full, inward, opposite)
        core = swapped(full, "core", 1)
        z2 = swapped(full, "z", 2)
        x2 = swapped(full, "rep", 1)
        y2 = swapped(full, "y", 2)
        second = across(jnp.where(on_first, first, full), outward, inward)
        x1 = swapped(after(full, first, core), "x_lo", 1)
        y1 = swapped(after(full, first, x2), "y", 1)
        z1 = swapped(after(full, first, y2), "z", 1)
        return {1: [core], 0: [x2], 3: [y2]}, {6: [first, second], 7: [second, first]}, {5: [z2], 8: [x1], 2: [y1], 4: [z1]}

    def call(body, parts, outs, scratch, *operands):
        held = []
        places = []
        for bit, arrays in parts.items():
            for array in arrays:
                if not any(array is other for other in held):
                    held.append(array)
            places.append((bit, tuple(next(i for i, x in enumerate(held) if x is array) for array in arrays)))
        arrays = (index, coef, couple, *operands, *held)
        counts = tuple(places)
        moved = sum(x.size * x.dtype.itemsize for x in (*arrays, *outs))
        return pl.pallas_call(
            lambda *refs: body(counts, *refs),
            out_shape=outs,
            in_specs=[in_smem, in_smem] + [in_vmem] * (len(arrays) - 2),
            out_specs=[in_vmem] * len(outs),
            scratch_shapes=[pltpu.VMEM((2, levels, levels), bfloat16), *scratch],
            cost_estimate=pl.CostEstimate(flops=len(parts) * 8 * levels**3, bytes_accessed=moved, transcendentals=0),
            compiler_params=pltpu.CompilerParams(vmem_limit_bytes=12 * 2**20),
        )(*arrays)

    rounded = jnp.stack([rho_real, rho_imag]).astype(bfloat16)
    near = jnp.where(rep == 0, rounded[:, 0], rounded[:, 1])
    away = jnp.where(rep == 0, rounded[:, 1], rounded[:, 0])
    far = swapped(away, "rep", 1)
    full = jnp.where(rep == 0, jnp.concatenate([near, far], axis=1), jnp.concatenate([far, near], axis=1))

    early, inner, late = exchange(full)
    (total,) = call(functools.partial(early_kernel, with_prior=False), early, [slope], [], ham, full)
    (total,) = call(add_kernel, inner, [slope], [], total)
    first, middle = call(middle_kernel, late, [slope, whole], [], full, total)

    early, inner, late = exchange(middle)
    (total,) = call(functools.partial(early_kernel, with_prior=True), early, [slope], [], ham, middle, first)
    (total,) = call(add_kernel, inner, [slope], [], total)
    near, away = call(last_kernel, late, [half_float, half], [pltpu.VMEM((2, levels, levels), float32)], total)
    far = swapped(away, "rep", 1).astype(float32)
    stay = 1.0 - step_size * decay + (0.5 * step_size * step_size) * decay * decay
    is_own = (jnp.arange(2) == rep)[:, None, None]
    outs = []
    for part, state in enumerate((rho_real, rho_imag)):
        change = jnp.where(is_own, near[part][None], far[part][None])
        outs.append(stay[:, None, None] * state + change)
    return tuple(outs)


def solution(mesh):
    axes = Mesh(mesh.devices.reshape(*hier_sizes, mesh.shape["rep"]), (*hier, "rep"))
    placed = (
        P(hier, "rep", None),
        P(hier, "rep", None),
        P(),
        P(),
        P(),
        P(),
        P(),
        P(hier, None),
        P(hier, None),
        P(hier, None),
    )
    return jax.shard_map(
        local,
        mesh=axes,
        in_specs=placed,
        out_specs=(P(hier, "rep", None), P(hier, "rep", None)),
        check_vma=False,
    )
```

```python
import functools

import jax
import jax.numpy as jnp
from jax import lax
from jax.experimental import pallas as pl
from jax.experimental.pallas import tpu as pltpu
from jax.sharding import Mesh, PartitionSpec as P

step_size = 0.1
half_step = 0.5 * step_size
float32 = jnp.float32
bfloat16 = jnp.bfloat16

hier = ("x_lo", "z", "y", "core")
hier_sizes = (2, 16, 4, 2)


def swapped(value, axis, distance):
    pairs = [(source, source ^ distance) for source in range(lax.axis_size(axis))]
    return lax.ppermute(value, axis, pairs)


def across(value, near_core, far_core):
    ring, cores = lax.axis_size("z"), lax.axis_size("core")
    pairs = []
    for source in range(ring):
        for core, target in enumerate((near_core, far_core)):
            if target is not None:
                pairs.append((source * cores + core, target(source) % ring * cores + core))
    return lax.ppermute(value, ("z", "core"), pairs)


def inward(source):
    return source ^ 4


def opposite(source):
    return source ^ 8


def outward(source):
    return source - 4 if not source & 4 else source + 4


def after(value, *earlier):
    return lax.optimization_barrier((value, *earlier))[0]


def dot(left, right):
    return jnp.dot(left, right, preferred_element_type=float32)


def add_term(total, matrix, real, imag, weight_a, weight_b):
    left_real = dot(matrix, real)
    right_real = dot(real, matrix)
    left_imag = dot(matrix, imag)
    right_imag = dot(imag, matrix)
    total[0] += weight_b * (left_real + right_real) + weight_a * (left_imag - right_imag)
    total[1] += weight_b * (left_imag + right_imag) - weight_a * (left_real - right_real)


def add_commutator(total, ham_ref, real, imag):
    ham_real, ham_imag = ham_ref[0], ham_ref[1]
    total[0] += dot(ham_real, imag) + dot(ham_imag, real) - dot(real, ham_imag) - dot(imag, ham_real)
    total[1] += dot(ham_imag, imag) - dot(ham_real, real) + dot(real, ham_real) - dot(imag, ham_imag)


def rows_of(first, count):
    return pl.ds(pl.multiple_of(first * count, count), count)


def add_bits(total, parts, index_ref, coef_ref, couple_ref, refs, whole):
    for bit, places in parts:
        source = refs[places[0]]
        if len(places) == 2:
            whole[...] = jnp.where(index_ref[10] == 0, source[...], refs[places[1]][...])
            source = whole
        matrix = couple_ref[index_ref[1 + bit]]
        add_term(total, matrix, source[0], source[1], coef_ref[0, bit], coef_ref[1, bit])


def early_kernel(parts, index_ref, coef_ref, couple_ref, ham_ref, own_ref, *refs, with_prior):
    if with_prior:
        prior_ref, *refs = refs
    *partner_refs, total, whole = refs
    if with_prior:
        total[...] = coef_ref[2, 0] * prior_ref[...]
    else:
        total[...] = jnp.zeros_like(total)
    add_commutator(total, ham_ref, own_ref[0], own_ref[1])
    add_bits(total, parts, index_ref, coef_ref, couple_ref, partner_refs, whole)


def add_kernel(parts, index_ref, coef_ref, couple_ref, total_ref, *refs):
    *partner_refs, out_ref, whole = refs
    out_ref[...] = total_ref[...]
    add_bits(out_ref, parts, index_ref, coef_ref, couple_ref, partner_refs, whole)


def middle_kernel(parts, index_ref, coef_ref, couple_ref, own_ref, total_ref, *refs):
    *partner_refs, slope_ref, middle_ref, whole = refs
    slope_ref[...] = total_ref[...]
    add_bits(slope_ref, parts, index_ref, coef_ref, couple_ref, partner_refs, whole)
    middle = coef_ref[2, 0] * own_ref[...].astype(float32) + step_size * slope_ref[...]
    middle_ref[...] = middle.astype(bfloat16)


def last_kernel(parts, index_ref, coef_ref, couple_ref, total_ref, *refs):
    *partner_refs, near_ref, far_ref, whole, total = refs
    total[...] = total_ref[...]
    add_bits(total, parts, index_ref, coef_ref, couple_ref, partner_refs, whole)
    near = index_ref[0]
    rows = near_ref.shape[1]
    near_ref[...] = half_step * total[:, rows_of(near, rows), :]
    far_ref[...] = (half_step * total[:, rows_of(1 - near, rows), :]).astype(bfloat16)


in_vmem = pl.BlockSpec(memory_space=pltpu.VMEM)
in_smem = pl.BlockSpec(memory_space=pltpu.SMEM)


def shaped(kind, *dims):
    return jax.ShapeDtypeStruct(dims, kind)


def local(rho_real, rho_imag, ham, couple, rates, coeff_real, coeff_imag, occupation, upper, lower):
    rep = lax.axis_index("rep")
    rows, levels = rho_real.shape[1:]
    bit_count = lax.axis_size(hier).bit_length()

    own_index = 2 * lax.axis_index(hier) + rep
    occ_float = occupation.astype(float32)
    decay = jnp.sum(occ_float * rates[None, :], axis=1)
    pick = lambda table: jnp.where(rep == 0, table[0], table[1])
    own_occ, own_up, own_low, own_decay = pick(occ_float), pick(upper), pick(lower), pick(decay)
    partner = jnp.bitwise_xor(own_index, jnp.left_shift(1, jnp.arange(bit_count, dtype=jnp.int32)))
    is_above = own_up[None, :] == partner[:, None]
    is_below = own_low[None, :] == partner[:, None]
    mode_range = jnp.arange(couple.shape[0], dtype=jnp.int32)
    modes = jnp.sum(jnp.where(is_above | is_below, mode_range[None, :], 0), axis=1)
    weight_a = jnp.sum(jnp.where(is_above, 1.0, jnp.where(is_below, (own_occ * coeff_real)[None, :], 0.0)), axis=1)
    weight_b = jnp.sum(jnp.where(is_below, (own_occ * coeff_imag)[None, :], 0.0), axis=1)
    keep = 1.0 - step_size * own_decay
    index = jnp.concatenate([rep[None], modes, lax.axis_index("core")[None]]).astype(jnp.int32)
    keeps = jnp.where(jnp.arange(bit_count) < 2, keep, 0.0)
    coef = jnp.stack([weight_a, weight_b, keeps]).astype(float32)

    on_first = lax.axis_index("core") == 0
    whole = shaped(bfloat16, 2, levels, levels)
    slope = shaped(float32, 2, levels, levels)
    half = shaped(bfloat16, 2, rows, levels)
    half_float = shaped(float32, 2, rows, levels)

    def exchange(full):
        first = across(full, inward, opposite)
        z1 = swapped(full, "z", 1)
        z2 = swapped(full, "z", 2)
        x2 = swapped(full, "rep", 1)
        y2 = swapped(full, "y", 2)
        second = across(jnp.where(on_first, first, full), outward, inward)
        x1 = swapped(after(full, first, z1), "x_lo", 1)
        y1 = swapped(after(full, first, x2), "y", 1)
        core = swapped(after(full, first, z2), "core", 1)
        return {4: [z1], 0: [x2], 3: [y2]}, {6: [first, second], 7: [second, first]}, {5: [z2], 8: [x1], 2: [y1], 1: [core]}

    def call(body, parts, outs, scratch, *operands):
        held = []
        places = []
        for bit, arrays in parts.items():
            for array in arrays:
                if not any(array is other for other in held):
                    held.append(array)
            places.append((bit, tuple(next(i for i, x in enumerate(held) if x is array) for array in arrays)))
        arrays = (index, coef, couple, *operands, *held)
        counts = tuple(places)
        moved = sum(x.size * x.dtype.itemsize for x in (*arrays, *outs))
        return pl.pallas_call(
            lambda *refs: body(counts, *refs),
            out_shape=outs,
            in_specs=[in_smem, in_smem] + [in_vmem] * (len(arrays) - 2),
            out_specs=[in_vmem] * len(outs),
            scratch_shapes=[pltpu.VMEM((2, levels, levels), bfloat16), *scratch],
            cost_estimate=pl.CostEstimate(flops=len(parts) * 8 * levels**3, bytes_accessed=moved, transcendentals=0),
            compiler_params=pltpu.CompilerParams(vmem_limit_bytes=12 * 2**20),
        )(*arrays)

    rounded = jnp.stack([rho_real, rho_imag]).astype(bfloat16)
    near = jnp.where(rep == 0, rounded[:, 0], rounded[:, 1])
    away = jnp.where(rep == 0, rounded[:, 1], rounded[:, 0])
    far = swapped(away, "rep", 1)
    full = jnp.where(rep == 0, jnp.concatenate([near, far], axis=1), jnp.concatenate([far, near], axis=1))

    early, inner, late = exchange(full)
    (total,) = call(functools.partial(early_kernel, with_prior=False), early, [slope], [], ham, full)
    (total,) = call(add_kernel, inner, [slope], [], total)
    first, middle = call(middle_kernel, late, [slope, whole], [], full, total)

    early, inner, late = exchange(middle)
    (total,) = call(functools.partial(early_kernel, with_prior=True), early, [slope], [], ham, middle, first)
    (total,) = call(add_kernel, inner, [slope], [], total)
    near, away = call(last_kernel, late, [half_float, half], [pltpu.VMEM((2, levels, levels), float32)], total)
    far = swapped(away, "rep", 1).astype(float32)
    stay = 1.0 - step_size * decay + (0.5 * step_size * step_size) * decay * decay
    is_own = (jnp.arange(2) == rep)[:, None, None]
    outs = []
    for part, state in enumerate((rho_real, rho_imag)):
        change = jnp.where(is_own, near[part][None], far[part][None])
        outs.append(stay[:, None, None] * state + change)
    return tuple(outs)


def solution(mesh):
    axes = Mesh(mesh.devices.reshape(*hier_sizes, mesh.shape["rep"]), (*hier, "rep"))
    placed = (
        P(hier, "rep", None),
        P(hier, "rep", None),
        P(),
        P(),
        P(),
        P(),
        P(),
        P(hier, None),
        P(hier, None),
        P(hier, None),
    )
    return jax.shard_map(
        local,
        mesh=axes,
        in_specs=placed,
        out_specs=(P(hier, "rep", None), P(hier, "rep", None)),
        check_vma=False,
    )
```

```python
import functools

import jax
import jax.numpy as jnp
from jax import lax
from jax.experimental import pallas as pl
from jax.experimental.pallas import tpu as pltpu
from jax.sharding import Mesh, PartitionSpec as P

step_size = 0.1
half_step = 0.5 * step_size
float32 = jnp.float32
bfloat16 = jnp.bfloat16

hier = ("x_lo", "z", "y", "core")
hier_sizes = (2, 16, 4, 2)


def swapped(value, axis, distance):
    pairs = [(source, source ^ distance) for source in range(lax.axis_size(axis))]
    return lax.ppermute(value, axis, pairs)


def across(value, near_core, far_core):
    ring, cores = lax.axis_size("z"), lax.axis_size("core")
    pairs = []
    for source in range(ring):
        for core, target in enumerate((near_core, far_core)):
            if target is not None:
                pairs.append((source * cores + core, target(source) % ring * cores + core))
    return lax.ppermute(value, ("z", "core"), pairs)


def inward(source):
    return source ^ 4


def opposite(source):
    return source ^ 8


def outward(source):
    return source - 4 if not source & 4 else source + 4


def after(value, *earlier):
    return lax.optimization_barrier((value, *earlier))[0]


def dot(left, right):
    return jnp.dot(left, right, preferred_element_type=float32)


def add_term(total, matrix, real, imag, weight_a, weight_b):
    left_real = dot(matrix, real)
    right_real = dot(real, matrix)
    left_imag = dot(matrix, imag)
    right_imag = dot(imag, matrix)
    total[0] += weight_b * (left_real + right_real) + weight_a * (left_imag - right_imag)
    total[1] += weight_b * (left_imag + right_imag) - weight_a * (left_real - right_real)


def add_commutator(total, ham_ref, real, imag):
    ham_real, ham_imag = ham_ref[0], ham_ref[1]
    total[0] += dot(ham_real, imag) + dot(ham_imag, real) - dot(real, ham_imag) - dot(imag, ham_real)
    total[1] += dot(ham_imag, imag) - dot(ham_real, real) + dot(real, ham_real) - dot(imag, ham_imag)


def rows_of(first, count):
    return pl.ds(pl.multiple_of(first * count, count), count)


def add_bits(total, parts, index_ref, coef_ref, couple_ref, refs, whole):
    for bit, places in parts:
        source = refs[places[0]]
        if len(places) == 2:
            whole[...] = jnp.where(index_ref[10] == 0, source[...], refs[places[1]][...])
            source = whole
        matrix = couple_ref[index_ref[1 + bit]]
        add_term(total, matrix, source[0], source[1], coef_ref[0, bit], coef_ref[1, bit])


def early_kernel(parts, index_ref, coef_ref, couple_ref, ham_ref, own_ref, *refs, with_prior):
    if with_prior:
        prior_ref, *refs = refs
    *partner_refs, total, whole = refs
    if with_prior:
        total[...] = coef_ref[2, 0] * prior_ref[...]
    else:
        total[...] = jnp.zeros_like(total)
    add_commutator(total, ham_ref, own_ref[0], own_ref[1])
    add_bits(total, parts, index_ref, coef_ref, couple_ref, partner_refs, whole)


def add_kernel(parts, index_ref, coef_ref, couple_ref, total_ref, *refs):
    *partner_refs, out_ref, whole = refs
    out_ref[...] = total_ref[...]
    add_bits(out_ref, parts, index_ref, coef_ref, couple_ref, partner_refs, whole)


def middle_kernel(parts, index_ref, coef_ref, couple_ref, own_ref, total_ref, *refs):
    *partner_refs, slope_ref, middle_ref, whole = refs
    slope_ref[...] = total_ref[...]
    add_bits(slope_ref, parts, index_ref, coef_ref, couple_ref, partner_refs, whole)
    middle = coef_ref[2, 0] * own_ref[...].astype(float32) + step_size * slope_ref[...]
    middle_ref[...] = middle.astype(bfloat16)


def last_kernel(parts, index_ref, coef_ref, couple_ref, total_ref, *refs):
    *partner_refs, near_ref, far_ref, whole, total = refs
    total[...] = total_ref[...]
    add_bits(total, parts, index_ref, coef_ref, couple_ref, partner_refs, whole)
    near = index_ref[0]
    rows = near_ref.shape[1]
    near_ref[...] = half_step * total[:, rows_of(near, rows), :]
    far_ref[...] = (half_step * total[:, rows_of(1 - near, rows), :]).astype(bfloat16)


in_vmem = pl.BlockSpec(memory_space=pltpu.VMEM)
in_smem = pl.BlockSpec(memory_space=pltpu.SMEM)


def shaped(kind, *dims):
    return jax.ShapeDtypeStruct(dims, kind)


def local(rho_real, rho_imag, ham, couple, rates, coeff_real, coeff_imag, occupation, upper, lower):
    rep = lax.axis_index("rep")
    rows, levels = rho_real.shape[1:]
    bit_count = lax.axis_size(hier).bit_length()

    own_index = 2 * lax.axis_index(hier) + rep
    occ_float = occupation.astype(float32)
    decay = jnp.sum(occ_float * rates[None, :], axis=1)
    pick = lambda table: jnp.where(rep == 0, table[0], table[1])
    own_occ, own_up, own_low, own_decay = pick(occ_float), pick(upper), pick(lower), pick(decay)
    partner = jnp.bitwise_xor(own_index, jnp.left_shift(1, jnp.arange(bit_count, dtype=jnp.int32)))
    is_above = own_up[None, :] == partner[:, None]
    is_below = own_low[None, :] == partner[:, None]
    mode_range = jnp.arange(couple.shape[0], dtype=jnp.int32)
    modes = jnp.sum(jnp.where(is_above | is_below, mode_range[None, :], 0), axis=1)
    weight_a = jnp.sum(jnp.where(is_above, 1.0, jnp.where(is_below, (own_occ * coeff_real)[None, :], 0.0)), axis=1)
    weight_b = jnp.sum(jnp.where(is_below, (own_occ * coeff_imag)[None, :], 0.0), axis=1)
    keep = 1.0 - step_size * own_decay
    index = jnp.concatenate([rep[None], modes, lax.axis_index("core")[None]]).astype(jnp.int32)
    keeps = jnp.where(jnp.arange(bit_count) < 2, keep, 0.0)
    coef = jnp.stack([weight_a, weight_b, keeps]).astype(float32)

    on_first = lax.axis_index("core") == 0
    whole = shaped(bfloat16, 2, levels, levels)
    slope = shaped(float32, 2, levels, levels)
    half = shaped(bfloat16, 2, rows, levels)
    half_float = shaped(float32, 2, rows, levels)

    def exchange(full):
        first = across(full, inward, opposite)
        z1 = swapped(full, "z", 1)
        z2 = swapped(full, "z", 2)
        x2 = swapped(full, "rep", 1)
        y2 = swapped(full, "y", 2)
        second = across(jnp.where(on_first, first, full), outward, inward)
        x1 = swapped(after(full, first, x2), "x_lo", 1)
        y1 = swapped(after(full, first, z1), "y", 1)
        core = swapped(after(full, first, z2), "core", 1)
        return {4: [z1], 0: [x2], 3: [y2]}, {6: [first, second], 7: [second, first]}, {5: [z2], 8: [x1], 2: [y1], 1: [core]}

    def call(body, parts, outs, scratch, *operands):
        held = []
        places = []
        for bit, arrays in parts.items():
            for array in arrays:
                if not any(array is other for other in held):
                    held.append(array)
            places.append((bit, tuple(next(i for i, x in enumerate(held) if x is array) for array in arrays)))
        arrays = (index, coef, couple, *operands, *held)
        counts = tuple(places)
        moved = sum(x.size * x.dtype.itemsize for x in (*arrays, *outs))
        return pl.pallas_call(
            lambda *refs: body(counts, *refs),
            out_shape=outs,
            in_specs=[in_smem, in_smem] + [in_vmem] * (len(arrays) - 2),
            out_specs=[in_vmem] * len(outs),
            scratch_shapes=[pltpu.VMEM((2, levels, levels), bfloat16), *scratch],
            cost_estimate=pl.CostEstimate(flops=len(parts) * 8 * levels**3, bytes_accessed=moved, transcendentals=0),
            compiler_params=pltpu.CompilerParams(vmem_limit_bytes=12 * 2**20),
        )(*arrays)

    rounded = jnp.stack([rho_real, rho_imag]).astype(bfloat16)
    near = jnp.where(rep == 0, rounded[:, 0], rounded[:, 1])
    away = jnp.where(rep == 0, rounded[:, 1], rounded[:, 0])
    far = swapped(away, "rep", 1)
    full = jnp.where(rep == 0, jnp.concatenate([near, far], axis=1), jnp.concatenate([far, near], axis=1))

    early, inner, late = exchange(full)
    (total,) = call(functools.partial(early_kernel, with_prior=False), early, [slope], [], ham, full)
    (total,) = call(add_kernel, inner, [slope], [], total)
    first, middle = call(middle_kernel, late, [slope, whole], [], full, total)

    early, inner, late = exchange(middle)
    (total,) = call(functools.partial(early_kernel, with_prior=True), early, [slope], [], ham, middle, first)
    (total,) = call(add_kernel, inner, [slope], [], total)
    near, away = call(last_kernel, late, [half_float, half], [pltpu.VMEM((2, levels, levels), float32)], total)
    far = swapped(away, "rep", 1).astype(float32)
    stay = 1.0 - step_size * decay + (0.5 * step_size * step_size) * decay * decay
    is_own = (jnp.arange(2) == rep)[:, None, None]
    outs = []
    for part, state in enumerate((rho_real, rho_imag)):
        change = jnp.where(is_own, near[part][None], far[part][None])
        outs.append(stay[:, None, None] * state + change)
    return tuple(outs)


def solution(mesh):
    axes = Mesh(mesh.devices.reshape(*hier_sizes, mesh.shape["rep"]), (*hier, "rep"))
    placed = (
        P(hier, "rep", None),
        P(hier, "rep", None),
        P(),
        P(),
        P(),
        P(),
        P(),
        P(hier, None),
        P(hier, None),
        P(hier, None),
    )
    return jax.shard_map(
        local,
        mesh=axes,
        in_specs=placed,
        out_specs=(P(hier, "rep", None), P(hier, "rep", None)),
        check_vma=False,
    )
```

```python
import functools

import jax
import jax.numpy as jnp
from jax import lax
from jax.experimental import pallas as pl
from jax.experimental.pallas import tpu as pltpu
from jax.sharding import Mesh, PartitionSpec as P

step_size = 0.1
half_step = 0.5 * step_size
float32 = jnp.float32
bfloat16 = jnp.bfloat16

hier = ("x_lo", "z", "y", "core")
hier_sizes = (2, 16, 4, 2)


def swapped(value, axis, distance):
    pairs = [(source, source ^ distance) for source in range(lax.axis_size(axis))]
    return lax.ppermute(value, axis, pairs)


def across(value, near_core, far_core):
    ring, cores = lax.axis_size("z"), lax.axis_size("core")
    pairs = []
    for source in range(ring):
        for core, target in enumerate((near_core, far_core)):
            if target is not None:
                pairs.append((source * cores + core, target(source) % ring * cores + core))
    return lax.ppermute(value, ("z", "core"), pairs)


def inward(source):
    return source ^ 4


def opposite(source):
    return source ^ 8


def outward(source):
    return source - 4 if not source & 4 else source + 4


def after(value, *earlier):
    return lax.optimization_barrier((value, *earlier))[0]


def dot(left, right):
    return jnp.dot(left, right, preferred_element_type=float32)


def add_term(total, matrix, real, imag, weight_a, weight_b):
    left_real = dot(matrix, real)
    right_real = dot(real, matrix)
    left_imag = dot(matrix, imag)
    right_imag = dot(imag, matrix)
    total[0] += weight_b * (left_real + right_real) + weight_a * (left_imag - right_imag)
    total[1] += weight_b * (left_imag + right_imag) - weight_a * (left_real - right_real)


def add_commutator(total, ham_ref, real, imag):
    ham_real, ham_imag = ham_ref[0], ham_ref[1]
    total[0] += dot(ham_real, imag) + dot(ham_imag, real) - dot(real, ham_imag) - dot(imag, ham_real)
    total[1] += dot(ham_imag, imag) - dot(ham_real, real) + dot(real, ham_real) - dot(imag, ham_imag)


def rows_of(first, count):
    return pl.ds(pl.multiple_of(first * count, count), count)


def add_bits(total, parts, index_ref, coef_ref, couple_ref, refs, whole):
    for bit, places in parts:
        source = refs[places[0]]
        if len(places) == 2:
            whole[...] = jnp.where(index_ref[10] == 0, source[...], refs[places[1]][...])
            source = whole
        matrix = couple_ref[index_ref[1 + bit]]
        add_term(total, matrix, source[0], source[1], coef_ref[0, bit], coef_ref[1, bit])


def early_kernel(parts, index_ref, coef_ref, couple_ref, ham_ref, own_ref, *refs, with_prior):
    if with_prior:
        prior_ref, *refs = refs
    *partner_refs, total, whole = refs
    if with_prior:
        total[...] = coef_ref[2, 0] * prior_ref[...]
    else:
        total[...] = jnp.zeros_like(total)
    add_commutator(total, ham_ref, own_ref[0], own_ref[1])
    add_bits(total, parts, index_ref, coef_ref, couple_ref, partner_refs, whole)


def middle_kernel(parts, index_ref, coef_ref, couple_ref, own_ref, total_ref, *refs):
    *partner_refs, slope_ref, middle_ref, whole = refs
    slope_ref[...] = total_ref[...]
    add_bits(slope_ref, parts, index_ref, coef_ref, couple_ref, partner_refs, whole)
    middle = coef_ref[2, 0] * own_ref[...].astype(float32) + step_size * slope_ref[...]
    middle_ref[...] = middle.astype(bfloat16)


def last_kernel(parts, index_ref, coef_ref, couple_ref, total_ref, *refs):
    *partner_refs, near_ref, far_ref, whole, total = refs
    total[...] = total_ref[...]
    add_bits(total, parts, index_ref, coef_ref, couple_ref, partner_refs, whole)
    near = index_ref[0]
    rows = near_ref.shape[1]
    near_ref[...] = half_step * total[:, rows_of(near, rows), :]
    far_ref[...] = (half_step * total[:, rows_of(1 - near, rows), :]).astype(bfloat16)


in_vmem = pl.BlockSpec(memory_space=pltpu.VMEM)
in_smem = pl.BlockSpec(memory_space=pltpu.SMEM)


def shaped(kind, *dims):
    return jax.ShapeDtypeStruct(dims, kind)


def local(rho_real, rho_imag, ham, couple, rates, coeff_real, coeff_imag, occupation, upper, lower):
    rep = lax.axis_index("rep")
    rows, levels = rho_real.shape[1:]
    bit_count = lax.axis_size(hier).bit_length()

    own_index = 2 * lax.axis_index(hier) + rep
    occ_float = occupation.astype(float32)
    decay = jnp.sum(occ_float * rates[None, :], axis=1)
    pick = lambda table: jnp.where(rep == 0, table[0], table[1])
    own_occ, own_up, own_low, own_decay = pick(occ_float), pick(upper), pick(lower), pick(decay)
    partner = jnp.bitwise_xor(own_index, jnp.left_shift(1, jnp.arange(bit_count, dtype=jnp.int32)))
    is_above = own_up[None, :] == partner[:, None]
    is_below = own_low[None, :] == partner[:, None]
    mode_range = jnp.arange(couple.shape[0], dtype=jnp.int32)
    modes = jnp.sum(jnp.where(is_above | is_below, mode_range[None, :], 0), axis=1)
    weight_a = jnp.sum(jnp.where(is_above, 1.0, jnp.where(is_below, (own_occ * coeff_real)[None, :], 0.0)), axis=1)
    weight_b = jnp.sum(jnp.where(is_below, (own_occ * coeff_imag)[None, :], 0.0), axis=1)
    keep = 1.0 - step_size * own_decay
    index = jnp.concatenate([rep[None], modes, lax.axis_index("core")[None]]).astype(jnp.int32)
    keeps = jnp.where(jnp.arange(bit_count) < 2, keep, 0.0)
    coef = jnp.stack([weight_a, weight_b, keeps]).astype(float32)

    on_first = lax.axis_index("core") == 0
    whole = shaped(bfloat16, 2, levels, levels)
    slope = shaped(float32, 2, levels, levels)
    half = shaped(bfloat16, 2, rows, levels)
    half_float = shaped(float32, 2, rows, levels)

    def exchange(full):
        first = across(full, inward, opposite)
        z1 = swapped(full, "z", 1)
        z2 = swapped(full, "z", 2)
        x2 = swapped(full, "rep", 1)
        y2 = swapped(full, "y", 2)
        second = across(jnp.where(on_first, first, full), outward, inward)
        x1 = swapped(after(full, first, x2), "x_lo", 1)
        y1 = swapped(after(full, first, z1), "y", 1)
        core = swapped(after(full, first, z2), "core", 1)
        return {4: [z1], 0: [x2], 3: [y2]}, {6: [first, second], 7: [second, first], 5: [z2], 8: [x1], 2: [y1], 1: [core]}

    def call(body, parts, outs, scratch, *operands):
        held = []
        places = []
        for bit, arrays in parts.items():
            for array in arrays:
                if not any(array is other for other in held):
                    held.append(array)
            places.append((bit, tuple(next(i for i, x in enumerate(held) if x is array) for array in arrays)))
        arrays = (index, coef, couple, *operands, *held)
        counts = tuple(places)
        moved = sum(x.size * x.dtype.itemsize for x in (*arrays, *outs))
        return pl.pallas_call(
            lambda *refs: body(counts, *refs),
            out_shape=outs,
            in_specs=[in_smem, in_smem] + [in_vmem] * (len(arrays) - 2),
            out_specs=[in_vmem] * len(outs),
            scratch_shapes=[pltpu.VMEM((2, levels, levels), bfloat16), *scratch],
            cost_estimate=pl.CostEstimate(flops=len(parts) * 8 * levels**3, bytes_accessed=moved, transcendentals=0),
            compiler_params=pltpu.CompilerParams(vmem_limit_bytes=12 * 2**20),
        )(*arrays)

    rounded = jnp.stack([rho_real, rho_imag]).astype(bfloat16)
    near = jnp.where(rep == 0, rounded[:, 0], rounded[:, 1])
    away = jnp.where(rep == 0, rounded[:, 1], rounded[:, 0])
    far = swapped(away, "rep", 1)
    full = jnp.where(rep == 0, jnp.concatenate([near, far], axis=1), jnp.concatenate([far, near], axis=1))

    early, late = exchange(full)
    (total,) = call(functools.partial(early_kernel, with_prior=False), early, [slope], [], ham, full)
    first, middle = call(middle_kernel, late, [slope, whole], [], full, total)

    early, late = exchange(middle)
    (total,) = call(functools.partial(early_kernel, with_prior=True), early, [slope], [], ham, middle, first)
    near, away = call(last_kernel, late, [half_float, half], [pltpu.VMEM((2, levels, levels), float32)], total)
    far = swapped(away, "rep", 1).astype(float32)
    stay = 1.0 - step_size * decay + (0.5 * step_size * step_size) * decay * decay
    is_own = (jnp.arange(2) == rep)[:, None, None]
    outs = []
    for part, state in enumerate((rho_real, rho_imag)):
        change = jnp.where(is_own, near[part][None], far[part][None])
        outs.append(stay[:, None, None] * state + change)
    return tuple(outs)


def solution(mesh):
    axes = Mesh(mesh.devices.reshape(*hier_sizes, mesh.shape["rep"]), (*hier, "rep"))
    placed = (
        P(hier, "rep", None),
        P(hier, "rep", None),
        P(),
        P(),
        P(),
        P(),
        P(),
        P(hier, None),
        P(hier, None),
        P(hier, None),
    )
    return jax.shard_map(
        local,
        mesh=axes,
        in_specs=placed,
        out_specs=(P(hier, "rep", None), P(hier, "rep", None)),
        check_vma=False,
    )
```

```python
import functools

import jax
import jax.numpy as jnp
from jax import lax
from jax.experimental import pallas as pl
from jax.experimental.pallas import tpu as pltpu
from jax.sharding import Mesh, PartitionSpec as P

step_size = 0.1
half_step = 0.5 * step_size
float32 = jnp.float32
bfloat16 = jnp.bfloat16

hier = ("x_lo", "z", "y", "core")
hier_sizes = (2, 16, 4, 2)


def swapped(value, axis, distance):
    pairs = [(source, source ^ distance) for source in range(lax.axis_size(axis))]
    return lax.ppermute(value, axis, pairs)


def across(value, near_core, far_core):
    ring, cores = lax.axis_size("z"), lax.axis_size("core")
    pairs = []
    for source in range(ring):
        for core, target in enumerate((near_core, far_core)):
            if target is not None:
                pairs.append((source * cores + core, target(source) % ring * cores + core))
    return lax.ppermute(value, ("z", "core"), pairs)


def inward(source):
    return source ^ 4


def opposite(source):
    return source ^ 8


def outward(source):
    return source - 4 if not source & 4 else source + 4


def after(value, *earlier):
    return lax.optimization_barrier((value, *earlier))[0]


def dot(left, right):
    return jnp.dot(left, right, preferred_element_type=float32)


def add_term(total, matrix, real, imag, weight_a, weight_b):
    left_real = dot(matrix, real)
    right_real = dot(real, matrix)
    left_imag = dot(matrix, imag)
    right_imag = dot(imag, matrix)
    total[0] += weight_b * (left_real + right_real) + weight_a * (left_imag - right_imag)
    total[1] += weight_b * (left_imag + right_imag) - weight_a * (left_real - right_real)


def add_commutator(total, ham_ref, real, imag):
    ham_real, ham_imag = ham_ref[0], ham_ref[1]
    total[0] += dot(ham_real, imag) + dot(ham_imag, real) - dot(real, ham_imag) - dot(imag, ham_real)
    total[1] += dot(ham_imag, imag) - dot(ham_real, real) + dot(real, ham_real) - dot(imag, ham_imag)


def rows_of(first, count):
    return pl.ds(pl.multiple_of(first * count, count), count)


def add_bits(total, parts, index_ref, coef_ref, couple_ref, refs, whole):
    for bit, places in parts:
        source = refs[places[0]]
        if len(places) == 2:
            whole[...] = jnp.where(index_ref[10] == 0, source[...], refs[places[1]][...])
            source = whole
        matrix = couple_ref[index_ref[1 + bit]]
        add_term(total, matrix, source[0], source[1], coef_ref[0, bit], coef_ref[1, bit])


def early_kernel(parts, index_ref, coef_ref, couple_ref, ham_ref, own_ref, *refs, with_prior):
    if with_prior:
        prior_ref, *refs = refs
    *partner_refs, total, whole = refs
    if with_prior:
        total[...] = coef_ref[2, 0] * prior_ref[...]
    else:
        total[...] = jnp.zeros_like(total)
    add_commutator(total, ham_ref, own_ref[0], own_ref[1])
    add_bits(total, parts, index_ref, coef_ref, couple_ref, partner_refs, whole)


def middle_kernel(parts, index_ref, coef_ref, couple_ref, own_ref, total_ref, *refs):
    *partner_refs, slope_ref, middle_ref, whole = refs
    slope_ref[...] = total_ref[...]
    add_bits(slope_ref, parts, index_ref, coef_ref, couple_ref, partner_refs, whole)
    middle = coef_ref[2, 0] * own_ref[...].astype(float32) + step_size * slope_ref[...]
    middle_ref[...] = middle.astype(bfloat16)


def last_kernel(parts, index_ref, coef_ref, couple_ref, total_ref, *refs):
    *partner_refs, near_ref, far_ref, whole, total = refs
    total[...] = total_ref[...]
    add_bits(total, parts, index_ref, coef_ref, couple_ref, partner_refs, whole)
    near = index_ref[0]
    rows = near_ref.shape[1]
    near_ref[...] = half_step * total[:, rows_of(near, rows), :]
    far_ref[...] = (half_step * total[:, rows_of(1 - near, rows), :]).astype(bfloat16)


in_vmem = pl.BlockSpec(memory_space=pltpu.VMEM)
in_smem = pl.BlockSpec(memory_space=pltpu.SMEM)


def shaped(kind, *dims):
    return jax.ShapeDtypeStruct(dims, kind)


def local(rho_real, rho_imag, ham, couple, rates, coeff_real, coeff_imag, occupation, upper, lower):
    rep = lax.axis_index("rep")
    rows, levels = rho_real.shape[1:]
    bit_count = lax.axis_size(hier).bit_length()

    own_index = 2 * lax.axis_index(hier) + rep
    occ_float = occupation.astype(float32)
    decay = jnp.sum(occ_float * rates[None, :], axis=1)
    pick = lambda table: jnp.where(rep == 0, table[0], table[1])
    own_occ, own_up, own_low, own_decay = pick(occ_float), pick(upper), pick(lower), pick(decay)
    partner = jnp.bitwise_xor(own_index, jnp.left_shift(1, jnp.arange(bit_count, dtype=jnp.int32)))
    is_above = own_up[None, :] == partner[:, None]
    is_below = own_low[None, :] == partner[:, None]
    mode_range = jnp.arange(couple.shape[0], dtype=jnp.int32)
    modes = jnp.sum(jnp.where(is_above | is_below, mode_range[None, :], 0), axis=1)
    weight_a = jnp.sum(jnp.where(is_above, 1.0, jnp.where(is_below, (own_occ * coeff_real)[None, :], 0.0)), axis=1)
    weight_b = jnp.sum(jnp.where(is_below, (own_occ * coeff_imag)[None, :], 0.0), axis=1)
    keep = 1.0 - step_size * own_decay
    index = jnp.concatenate([rep[None], modes, lax.axis_index("core")[None]]).astype(jnp.int32)
    keeps = jnp.where(jnp.arange(bit_count) < 2, keep, 0.0)
    coef = jnp.stack([weight_a, weight_b, keeps]).astype(float32)

    on_first = lax.axis_index("core") == 0
    whole = shaped(bfloat16, 2, levels, levels)
    slope = shaped(float32, 2, levels, levels)
    half = shaped(bfloat16, 2, rows, levels)
    half_float = shaped(float32, 2, rows, levels)

    def exchange(full):
        first = across(full, inward, opposite)
        z1 = swapped(full, "z", 1)
        z2 = swapped(full, "z", 2)
        x2 = swapped(full, "rep", 1)
        y2 = swapped(full, "y", 2)
        second = across(jnp.where(on_first, first, full), outward, inward)
        x1 = swapped(after(full, first, x2), "x_lo", 1)
        y1 = swapped(after(full, first, y2), "y", 1)
        core = swapped(after(full, first, z2, z1), "core", 1)
        return {4: [z1], 0: [x2], 3: [y2]}, {6: [first, second], 7: [second, first], 5: [z2], 8: [x1], 2: [y1], 1: [core]}

    def call(body, parts, outs, scratch, *operands):
        held = []
        places = []
        for bit, arrays in parts.items():
            for array in arrays:
                if not any(array is other for other in held):
                    held.append(array)
            places.append((bit, tuple(next(i for i, x in enumerate(held) if x is array) for array in arrays)))
        arrays = (index, coef, couple, *operands, *held)
        counts = tuple(places)
        moved = sum(x.size * x.dtype.itemsize for x in (*arrays, *outs))
        return pl.pallas_call(
            lambda *refs: body(counts, *refs),
            out_shape=outs,
            in_specs=[in_smem, in_smem] + [in_vmem] * (len(arrays) - 2),
            out_specs=[in_vmem] * len(outs),
            scratch_shapes=[pltpu.VMEM((2, levels, levels), bfloat16), *scratch],
            cost_estimate=pl.CostEstimate(flops=len(parts) * 8 * levels**3, bytes_accessed=moved, transcendentals=0),
            compiler_params=pltpu.CompilerParams(vmem_limit_bytes=12 * 2**20),
        )(*arrays)

    rounded = jnp.stack([rho_real, rho_imag]).astype(bfloat16)
    near = jnp.where(rep == 0, rounded[:, 0], rounded[:, 1])
    away = jnp.where(rep == 0, rounded[:, 1], rounded[:, 0])
    far = swapped(away, "rep", 1)
    full = jnp.where(rep == 0, jnp.concatenate([near, far], axis=1), jnp.concatenate([far, near], axis=1))

    early, late = exchange(full)
    (total,) = call(functools.partial(early_kernel, with_prior=False), early, [slope], [], ham, full)
    first, middle = call(middle_kernel, late, [slope, whole], [], full, total)

    early, late = exchange(middle)
    (total,) = call(functools.partial(early_kernel, with_prior=True), early, [slope], [], ham, middle, first)
    near, away = call(last_kernel, late, [half_float, half], [pltpu.VMEM((2, levels, levels), float32)], total)
    far = swapped(away, "rep", 1).astype(float32)
    stay = 1.0 - step_size * decay + (0.5 * step_size * step_size) * decay * decay
    is_own = (jnp.arange(2) == rep)[:, None, None]
    outs = []
    for part, state in enumerate((rho_real, rho_imag)):
        change = jnp.where(is_own, near[part][None], far[part][None])
        outs.append(stay[:, None, None] * state + change)
    return tuple(outs)


def solution(mesh):
    axes = Mesh(mesh.devices.reshape(*hier_sizes, mesh.shape["rep"]), (*hier, "rep"))
    placed = (
        P(hier, "rep", None),
        P(hier, "rep", None),
        P(),
        P(),
        P(),
        P(),
        P(),
        P(hier, None),
        P(hier, None),
        P(hier, None),
    )
    return jax.shard_map(
        local,
        mesh=axes,
        in_specs=placed,
        out_specs=(P(hier, "rep", None), P(hier, "rep", None)),
        check_vma=False,
    )
```
